32 devices in a mesh: groups: 2 (over x), tiles: 16 (over z, y, core).
Axes of the slice: x: 2, y: 2, z: 4, core: 2. Of those that a mesh axis runs over, the one named last changes fastest.
Arguments:
- tokens: bfloat16 [64, 512, 1664], P(('groups', 'tiles')), parts along dimension 0, may hold values from -16 to 16
- padding: int32 [64, 512], P('groups'), parts along dimension 0, may hold values from 0 to 1, as said below
- plan: int32 [32], P('groups'), parts along dimension 0, may hold values from 0 to 31, as said below
- neighbours: int32 [64, 4], P('groups'), parts along dimension 0, may hold values from -1 to 31, as said below
- norm_gain: float32 [1664], replicated, may hold values from 0.1 to 1.9
- attention_weight: bfloat16 [1664, 2496], P('tiles'), may hold values from -32 to 32
- output_weight: bfloat16 [832, 1664], P(None, 'tiles'), may hold values from -0.21875 to 0.21875
Outputs:
- attended: bfloat16 [64, 512, 1664], P(('groups', 'tiles')), parts along dimension 0
The draws below stay inside these ranges and needn't reach their ends.
There are 2 independent parts, one for each index of `groups`. The reference program is written for one: setup_inputs(seed, part) draws one part's arguments, and reference() takes and returns one part's arrays. A program takes and returns all parts, laid end to end along the dimension named above; an argument that names none is the same for every part. Nothing has to cross between parts.
Inputs may be any that keep to these rules, and one draw needn't show every extreme that they name: Distinct slots; the slots that plan names are exactly those that hold a half tile of a page. `neighbours`: -1 where a half tile has no neighbour on that side and in every row of a slot that holds none; relations are mutual (left with right, upper with lower) and join only half tiles of one page; a page is a grid of half tiles up to 6 across and up to 48 in all, whose last row may be incomplete. `padding`: in each slot, 1 for a first run of tokens in row-major order and 0 after it; at least half of each slot is 1.
All inputs are finite; a program needn't handle non-finite values.
Results may differ from the reference program's by a relative error of at most 0.012.
The reference program's roundings to bfloat16 on the way (of `normed`, `memory`, `prob` and `mixed`) count: a program that leaves them out, or rounds other values in their place, can miss the bound.
Values may be sent and summed in bfloat16 or wider, within the bound.
No kernel may reach another device: no remote copies, remote signals or barrier semaphores. Data moves between devices by JAX's collectives and lax.ppermute only.
A program may use at most 128 MiB of HBM per device.

```python
import math
import jax
import jax.numpy as jnp
from jax import lax

D = 1664
HEADS = 8
HS = 104
SIDE = 32
HOLD = 2
HALF = 16
HW = 832
RIM = 4
ROWS = 512
STRIP = 128
TILES = 16
N_TILES = 16


def page_layout(key):
    first_key, second_key, third_key, fourth_key = jax.random.split(key, 4)
    slot_count = HOLD * N_TILES
    shuffled = jax.random.permutation(first_key, slot_count).astype(jnp.int32)
    widths = jax.random.randint(second_key, (N_TILES,), 1, 7).astype(jnp.int32)
    tile_rows = 1 + jax.random.randint(third_key, (N_TILES,), 0, 24).astype(jnp.int32) % (24 // widths)
    widths = widths.at[0].set(6)
    tile_rows = tile_rows.at[0].set(4)
    areas = widths * 2 * tile_rows
    ends = jnp.cumsum(areas).astype(jnp.int32)
    tile = jnp.arange(N_TILES, dtype=jnp.int32)
    page = jnp.sum((ends[None, :] <= tile[:, None]).astype(jnp.int32), 1)
    start = ends[page] - areas[page]
    width = widths[page]
    finish = jnp.minimum(ends[page], N_TILES)
    inner = tile - start
    column = inner % width
    row = inner // width
    left = jnp.where(column > 0, tile - 1, -1)
    right = jnp.where((column < width - 1) & (tile + 1 < finish), tile + 1, -1)
    upper = jnp.where(row > 0, tile - width, -1)
    lower = jnp.where(tile + width < finish, tile + width, -1)
    beside = jnp.stack([left, right, upper, lower], 1)
    beside_slots = jnp.where(beside >= 0, shuffled[jnp.maximum(beside, 0)], -1).astype(jnp.int32)
    table = jnp.full((slot_count, 4), -1, jnp.int32).at[shuffled[:N_TILES]].set(beside_slots)
    placement = jax.random.permutation(fourth_key, N_TILES)
    plan = shuffled[:N_TILES][placement].astype(jnp.int32)
    return (plan, table)


def draw_plan(key, part):
    plan, table = page_layout(key)
    return plan


def draw_neighbours(key, part):
    plan, table = page_layout(key)
    return table


def draw_padding(key, part):
    key = jax.random.fold_in(key, 3)
    filled = jax.random.randint(key, (HOLD * N_TILES,), ROWS // 2, ROWS + 1)
    return (jnp.arange(ROWS)[None, :] < filled[:, None]).astype(jnp.int32)


def draw_tokens(key, part):
    key = jax.random.fold_in(key, 7)
    column_key, row_key, base_key = jax.random.split(key, 3)
    slot_count = HOLD * N_TILES
    columns = jnp.exp(jax.random.uniform(column_key, (D,), jnp.float32, 0.0, math.log(10.0)))
    rows = jnp.exp(jax.random.uniform(row_key, (slot_count, ROWS, 1), jnp.float32, 0.0, math.log(10.0)))
    values = jax.random.normal(base_key, (slot_count, ROWS, D), jnp.float32)
    return jnp.clip(0.1 * values * columns[None, None, :] * rows, -16.0, 16.0).astype(jnp.bfloat16)


def draw_attention_weight(key, part):
    key = jax.random.fold_in(key, 11)
    base_key = jax.random.fold_in(key, 0)
    base = jnp.clip(jax.random.normal(base_key, (D, 3 * HW), jnp.float32), -6.0, 6.0) * (1.0 / math.sqrt(D))
    return base.astype(jnp.bfloat16)


def block_scale(rng, shape, cuts, low, top_value):
    factor_of = 1.0
    for position, blocks in cuts:
        steps = jax.random.uniform(jax.random.fold_in(jax.random.fold_in(rng, 6), position), (blocks,), jnp.float32, low / len(cuts), top_value / len(cuts))
        factor_of = factor_of * jnp.repeat(jnp.exp(steps), shape[position] // blocks).reshape((-1,) + (1,) * (len(shape) - 1 - position))
    return factor_of


def normal_values(own_key, extent, deviation, limit, cuts=(), held_as=jnp.bfloat16):
    values = deviation * jax.random.normal(own_key, extent, jnp.float32)
    if cuts:
        values = values * block_scale(own_key, extent, cuts, -0.22, 0.18)
    return jnp.clip(values, -limit, limit).astype(held_as)


def setup_inputs(seed: int = 0, part: int = 0) -> dict:
    splits = jax.random.split(jax.random.key(seed), 8)
    part_splits = jax.random.split(jax.random.fold_in(splits[7], part), 8)
    return {
        "tokens": draw_tokens(jax.random.fold_in(jax.random.fold_in(splits[7], part), 71), part),
        "padding": draw_padding(jax.random.fold_in(jax.random.fold_in(splits[7], part), 71), part),
        "plan": draw_plan(jax.random.fold_in(jax.random.fold_in(splits[7], part), 71), part),
        "neighbours": draw_neighbours(jax.random.fold_in(jax.random.fold_in(splits[7], part), 71), part),
        "norm_gain": jnp.clip(1.0 + 0.18 * jax.random.normal(splits[4], (D,), jnp.float32), 0.1, 1.9),
        "attention_weight": draw_attention_weight(jax.random.fold_in(splits[7], 71), part),
        "output_weight": normal_values(splits[6], (HW, D), HW ** -0.5, 0.21875, ((1, 16),)),
    }


def normalize(inputs, scaling):
    values = inputs.astype(jnp.float32)
    center = lax.optimization_barrier(jnp.mean(values, -1, keepdims=True))
    offset = values - center
    spread = lax.optimization_barrier(jnp.mean(offset * offset, -1, keepdims=True))
    return (offset * lax.rsqrt(spread + 1e-06) * scaling.astype(jnp.float32)).astype(jnp.bfloat16)

def edge_rims(grid):
    trailing = grid.shape[1:]
    square = grid.reshape((HALF, SIDE) + trailing)
    band = 2 * RIM
    pieces = [square[:, SIDE - band:], square[:, :band], square[HALF - RIM:], square[:RIM]]
    return jnp.stack([block.reshape((STRIP,) + trailing) for block in pieces], 0)

def attend(query, keys, values, key_live):
    split_query = query.astype(jnp.float32).reshape(query.shape[0], HEADS, HS)
    split_keys = keys.astype(jnp.float32).reshape(keys.shape[0], HEADS, HS)
    split_values = values.astype(jnp.float32).reshape(values.shape[0], HEADS, HS)
    scores = jnp.einsum('qhd,khd->hqk', split_query, split_keys) * (1.0 / math.sqrt(HS))
    usable = key_live[None, None, :] > 0.5
    highest = lax.optimization_barrier(jnp.max(jnp.where(usable, scores, -1e+30), -1, keepdims=True))
    weights = jnp.where(usable, jnp.exp(scores - highest), 0.0)
    prob = (weights / lax.optimization_barrier(jnp.sum(weights, -1, keepdims=True))).astype(jnp.bfloat16)
    mixed = jnp.einsum('hqk,khd->qhd', prob.astype(jnp.float32), split_values)
    return mixed.astype(jnp.bfloat16).reshape(query.shape[0], HW)

def reference(tokens, padding, plan, neighbours, norm_gain, attention_weight, output_weight):
    slot_count = tokens.shape[0]
    slot_numbers = jnp.arange(slot_count, dtype=jnp.int32)
    matches = plan[None, :] == slot_numbers[:, None]
    live = jnp.any(matches, 1)
    order = lax.optimization_barrier(jnp.sum(jnp.where(matches, jnp.arange(TILES, dtype=jnp.int32)[None, :], 0), 1)).astype(jnp.int32)

    def project(slot):
        normed = normalize(tokens[slot], norm_gain)
        return jnp.dot(normed, attention_weight, preferred_element_type=jnp.float32).astype(jnp.bfloat16)
    memory = lax.map(project, plan)
    live_rows = padding.astype(jnp.float32)

    def one_tile(index):
        slot = plan[index]
        beside = neighbours[slot]
        present = beside >= 0
        safe = jnp.maximum(beside, 0)
        own = memory[index]
        rim_memory = []
        rim_live = []
        for side in range(4):
            rim_memory.append(edge_rims(memory[order[safe[side]]][:, HW:])[side])
            rim_live.append(edge_rims(live_rows[safe[side]])[side] * present[side].astype(jnp.float32))
        keys_all = jnp.concatenate([own[:, HW:]] + rim_memory, 0)
        live_all = jnp.concatenate([live_rows[slot]] + rim_live, 0)
        mixed = attend(own[:, :HW], keys_all[:, :HW], keys_all[:, HW:], live_all)
        return jnp.dot(mixed, output_weight, preferred_element_type=jnp.float32).astype(jnp.bfloat16)
    results = lax.map(one_tile, jnp.arange(TILES, dtype=jnp.int32))
    placed = results[order]
    return jnp.where(live[:, None, None], placed, jnp.zeros_like(placed))
```

```python
import functools
import math

import jax
import jax.numpy as jnp
from jax import lax
from jax.experimental import pallas as pl
from jax.experimental.pallas import tpu as pltpu
from jax.sharding import PartitionSpec as P

HEADS = 8
HS = 104
SIDE = 32
HALF = 16
RIM = 4
ROWS = 512
STRIP = 128
HW = HEADS * HS
BF = jnp.bfloat16

ROUND, SEND, BESIDE, HAS, TAKE, SLOT, MOVE, COUNT, KEEP = 0, 4, 8, 12, 16, 20, 21, 22, 23
INFO = 24


def routing(count, plan_ref, beside_ref, me_ref, out_ref, live, mate, stack):
    me = me_ref[0]

    def clear(s, _):
        live[s] = 0
        return 0

    lax.fori_loop(0, 2 * count, clear, 0)

    def mark(j, _):
        live[plan_ref[j]] = 1
        return 0

    lax.fori_loop(0, count, mark, 0)

    def match(t, depth):
        over = live[2 * t] + live[2 * t + 1] - 1
        mate[t] = t
        opposite = over * depth < 0
        top = jnp.maximum(jnp.abs(depth) - 1, 0)

        @pl.when(opposite)
        def _():
            other = stack[top]
            mate[t] = other
            mate[other] = t

        @pl.when((over != 0) & jnp.logical_not(opposite))
        def _():
            stack[jnp.abs(depth)] = t

        return depth + over

    lax.fori_loop(0, count, match, jnp.int32(0))

    def host(s):
        t = lax.shift_right_logical(s, 1)
        odd = jnp.bitwise_and(s, 1)
        moved = (odd == 1) & (live[2 * t] == 1)
        return jnp.where(moved, mate[t], t)

    first, second = live[2 * me], live[2 * me + 1]
    total = first + second
    keep = jnp.where(first == 1, 0, second)
    slot = jnp.where(total == 0, 2 * mate[me] + 1, 2 * me + keep)

    def walk(side):
        def more(state):
            return state[1] >= 0

        def step(state):
            return state[0] + 1, beside_ref[4 * state[1] + side]

        return lax.while_loop(more, step, (jnp.int32(0), beside_ref[4 * slot + side]))[0]

    column = jnp.bitwise_and(walk(0), 1)
    row = jnp.bitwise_and(walk(2), 1)
    for k in range(4):
        if k < 2:
            side = jnp.where(column == k, 1, 0)
        else:
            side = jnp.where(row == k - 2, 3, 2)
        other = beside_ref[4 * slot + side]
        has = other >= 0
        safe = jnp.maximum(other, 0)
        out_ref[ROUND + k] = jnp.where(has, jnp.bitwise_xor(host(safe), me), 0)
        out_ref[SEND + k] = jnp.bitwise_xor(side, 1)
        out_ref[BESIDE + k] = safe
        out_ref[HAS + k] = has.astype(jnp.int32)
        out_ref[TAKE + k] = side
    out_ref[SLOT] = slot
    out_ref[MOVE] = jnp.bitwise_xor(mate[me], me)
    out_ref[COUNT] = total
    out_ref[KEEP] = keep


def route(plan, neighbours, position):
    count = plan.shape[0]
    smem = pl.BlockSpec(memory_space=pltpu.SMEM)
    return pl.pallas_call(
        functools.partial(routing, count),
        out_shape=jax.ShapeDtypeStruct((INFO,), jnp.int32),
        in_specs=[smem] * 3,
        out_specs=smem,
        scratch_shapes=[
            pltpu.SMEM((2 * count,), jnp.int32),
            pltpu.SMEM((count,), jnp.int32),
            pltpu.SMEM((count + 1,), jnp.int32),
        ],
        name="routing",
    )(plan, neighbours.reshape(-1), position.reshape(1))


def normalize(inputs, scaling):
    values = inputs.astype(jnp.float32)
    center = jnp.mean(values, -1, keepdims=True)
    offset = values - center
    spread = jnp.mean(offset * offset, -1, keepdims=True)
    return (offset * lax.rsqrt(spread + 1e-06) * scaling).astype(BF)


def edge_rims(grid):
    trailing = grid.shape[1:]
    square = grid.reshape((HALF, SIDE) + trailing)
    band = 2 * RIM
    pieces = [square[:, SIDE - band :], square[:, :band], square[HALF - RIM :], square[:RIM]]
    return jnp.stack([block.reshape((STRIP,) + trailing) for block in pieces], 0)


def attend_kernel(heads, q_ref, own_ref, rim_ref, live_ref, out_ref):
    usable = live_ref[...] > 0.5
    factor = math.log2(math.e) / math.sqrt(HS)
    dims = (((1,), (1,)), ((), ()))
    for index, h in enumerate(heads):
        span = slice(h * HS, (h + 1) * HS)
        vspan = slice(HW + h * HS, HW + (h + 1) * HS)
        query = q_ref[:, span]
        keys = jnp.concatenate([own_ref[:, span], rim_ref[:, span]], 0)
        values = jnp.concatenate([own_ref[:, vspan], rim_ref[:, vspan]], 0)
        scores = lax.dot_general(query, keys, dims, preferred_element_type=jnp.float32)
        scores = jnp.where(usable, scores * factor, -1e30)
        weights = jnp.exp2(scores - jnp.max(scores, -1, keepdims=True))
        prob = (weights * (1.0 / jnp.sum(weights, -1, keepdims=True))).astype(BF)
        mixed = jnp.dot(prob, values, preferred_element_type=jnp.float32)
        out_ref[:, index * HS : (index + 1) * HS] = mixed.astype(BF)


def attend(query, own, rim, live, heads):
    rows = query.shape[0]
    keys = own.shape[0] + rim.shape[0]
    vmem = pl.BlockSpec(memory_space=pltpu.VMEM)
    return pl.pallas_call(
        functools.partial(attend_kernel, heads),
        out_shape=jax.ShapeDtypeStruct((rows, len(heads) * HS), BF),
        in_specs=[vmem] * 4,
        out_specs=vmem,
        compiler_params=pltpu.CompilerParams(vmem_limit_bytes=48 * 1024 * 1024),
        cost_estimate=pl.CostEstimate(
            flops=len(heads) * 4 * rows * keys * 256,
            bytes_accessed=4 * rows * HW * 5,
            transcendentals=len(heads) * rows * keys,
        ),
        name="attend",
    )(query, own, rim, live)


def ring_pairs(count):
    chips = count // 2
    order = list(range(0, chips, 2)) + list(range(chips - 1 - chips % 2, 0, -2))
    forward = []
    for index, chip in enumerate(order):
        after = order[(index + 1) % chips]
        forward += [(2 * chip + c, 2 * after + c) for c in range(2)]
    return order, forward


def gather_rows(piece, position, count):
    chips = count // 2
    if chips > 8:
        return lax.all_gather(piece, "tiles", axis=0, tiled=True)
    order, forward = ring_pairs(count)
    backward = [(b, a) for a, b in forward]
    swap = [(t, t ^ 1) for t in range(count)]
    order_table = jnp.array(order, jnp.int32)
    rank_table = jnp.array([order.index(c) for c in range(chips)], jnp.int32)
    rank = rank_table[position // 2]
    core = position % 2
    rows = piece.shape[0]
    full = jnp.zeros((count,) + piece.shape, piece.dtype)

    def put(full, block, step, start=0):
        chip = order_table[(rank + step + chips) % chips]
        peer = lax.ppermute(block, "tiles", swap)
        for data, c in ((block, core), (peer, 1 - core)):
            full = lax.dynamic_update_slice(full, data[None], (2 * chip + c, start, 0))
        return full

    full = put(full, piece, 0)
    ahead = behind = piece
    for step in range(1, chips // 2 + 1):
        if 2 * step < chips:
            ahead = lax.ppermute(ahead, "tiles", forward)
            behind = lax.ppermute(behind, "tiles", backward)
            full = put(full, ahead, -step)
            full = put(full, behind, step)
        else:
            cut = rows // 16 * 8
            ahead = lax.ppermute(ahead[:cut], "tiles", forward)
            behind = lax.ppermute(behind[cut:], "tiles", backward)
            full = put(full, ahead, step)
            full = put(full, behind, step, cut)
    return full.reshape(count * rows, piece.shape[1])


def meet(choice, block, count, otherwise):
    def branch(r):
        pairs = [(t, t ^ r) for t in range(count) if t ^ r < count]
        return lambda items: lax.ppermute(items[0], "tiles", pairs)

    branches = [lambda items: items[1]] + [branch(r) for r in range(1, count)]
    return lax.switch(choice, branches, (block, otherwise))


def shards(tokens, padding, plan, neighbours, norm_gain, attention_weight, output_weight):
    count = lax.axis_size("tiles")
    position = lax.axis_index("tiles")
    info = route(plan, neighbours, position)

    key_weight = gather_rows(attention_weight[:, HW:], position, count)
    query_weight = gather_rows(attention_weight[:, :HW], position, count)
    out_weight = gather_rows(output_weight.T, position, count)

    kept = lax.dynamic_index_in_dim(tokens, info[KEEP], 0, keepdims=False)
    got = meet(info[MOVE], tokens[1], count, kept)
    work = jnp.where(info[COUNT] == 0, got, kept)
    normed = normalize(work, norm_gain)
    strips = edge_rims(normed)
    nothing = jnp.zeros((STRIP, normed.shape[1]), BF)
    lives = [padding[info[SLOT]]]
    for k in range(4):
        beside = edge_rims(padding[info[BESIDE + k]])
        lives.append(beside[info[TAKE + k]] * info[HAS + k])
    live = jnp.concatenate(lives, 0).astype(jnp.float32)[None, :]

    def exchange(k):
        block = lax.dynamic_index_in_dim(strips, info[SEND + k], 0, keepdims=False)
        return meet(info[ROUND + k], block, count, nothing)

    if count > 16:
        rim_rows = lax.map(exchange, jnp.arange(4, dtype=jnp.int32)).reshape(4 * STRIP, -1)
    else:
        rim_rows = jnp.concatenate([exchange(k) for k in range(4)], 0)

    def dot(a, b):
        return jnp.dot(a, b, preferred_element_type=jnp.float32).astype(BF)

    own_keys = dot(normed, key_weight)
    rim_keys = dot(rim_rows, key_weight)
    query = dot(normed, query_weight)
    parts = [attend(query, own_keys, rim_keys, live, range(h, h + 2)) for h in range(0, HEADS, 2)]
    mixed = jnp.concatenate(parts, 1)
    back = meet(info[MOVE], mixed, count, mixed)
    total, keep = info[COUNT], info[KEEP]
    none = jnp.zeros_like(mixed)
    first = jnp.where((total > 0) & (keep == 0), mixed, none)
    second = jnp.where(total == 2, back, jnp.where((total == 1) & (keep == 1), mixed, none))
    both = jnp.concatenate([first, second], 0)
    result = lax.dot_general(
        both, out_weight, (((1,), (1,)), ((), ())), preferred_element_type=jnp.float32
    ).astype(BF)
    return result.reshape(tokens.shape)


def solution(mesh):
    return jax.shard_map(
        shards,
        mesh=mesh,
        in_specs=(
            P(("groups", "tiles"), None, None),
            P("groups", None),
            P("groups"),
            P("groups", None),
            P(),
            P("tiles", None),
            P(None, "tiles"),
        ),
        out_specs=P(("groups", "tiles"), None, None),
        check_vma=False,
    )
```

```python
import functools
import math

import jax
import jax.numpy as jnp
from jax import lax
from jax.experimental import pallas as pl
from jax.experimental.pallas import tpu as pltpu
from jax.sharding import PartitionSpec as P

HEADS = 8
HS = 104
HW = HEADS * HS
SIDE = 32
HALF = 16
RIM = 4
ROWS = 512
STRIP = 128
KEYS = ROWS + 4 * STRIP
HOLD = 2
LEAD = 64
BF = jnp.bfloat16

ROUNDS, MOST = 8, 15
MEET, SEND, SOURCE, LIVE, LATE, CORE, PLACE = 0, 16, 32, 40, 42, 43, 44
LOCAL, NONE = 16, 32


def routing(count, rows, plan_ref, beside_ref, me_ref, padding_ref, out_ref, mask_ref, live, used, color):
    me = me_ref[0]
    slots = HOLD * count

    def clear(s, _):
        live[s] = 0
        return 0

    lax.fori_loop(0, slots, clear, 0)

    def mark(j, _):
        live[plan_ref[j]] = 1
        return 0

    lax.fori_loop(0, count, mark, 0)

    def empty(t, _):
        used[t] = 0
        return 0

    lax.fori_loop(0, count, empty, 0)

    for weight in (2, 1, 0):

        def edge(e, _, weight=weight):
            s = lax.shift_right_logical(e, 1)
            side = 1 + 2 * jnp.bitwise_and(e, 1)
            n = beside_ref[4 * s + side]
            safe = jnp.maximum(n, 0)
            a, b = lax.shift_right_logical(s, 1), lax.shift_right_logical(safe, 1)
            heavy = live[2 * a] * live[2 * a + 1] + live[2 * b] * live[2 * b + 1]

            @pl.when((n >= 0) & (a != b) & (heavy == weight))
            def _():
                taken = jnp.bitwise_or(used[a], used[b])
                first = lax.while_loop(
                    lambda c: jnp.bitwise_and(lax.shift_right_logical(taken, c), 1) == 1,
                    lambda c: c + 1,
                    jnp.int32(0),
                )
                bit = lax.shift_left(jnp.int32(1), first)
                used[a] = jnp.bitwise_or(used[a], bit)
                used[b] = jnp.bitwise_or(used[b], bit)
                color[4 * s + side] = first
                color[4 * safe + jnp.bitwise_xor(side, 1)] = first

            return 0

        lax.fori_loop(0, 2 * slots, edge, 0)

    for r in range(MOST + 1):
        out_ref[MEET + r] = 0
        out_ref[SEND + r] = 0
    out_ref[LATE] = 0
    for i in range(HOLD):
        slot = HOLD * me + i
        out_ref[LIVE + i] = live[slot]
        mask_ref[i : i + 1, :ROWS] = padding_ref[pl.ds(slot, 1), :].astype(jnp.float32)
        for side in range(4):
            n = beside_ref[4 * slot + side]
            has = (n >= 0) & (live[slot] == 1)
            safe = jnp.maximum(n, 0)
            other = lax.shift_right_logical(safe, 1)
            away = has & (other != me)
            out_ref[SOURCE + 4 * i + side] = jnp.where(has, LOCAL + 4 * jnp.bitwise_and(safe, 1) + side, NONE)

            @pl.when(away)
            def _(i=i, side=side, slot=slot, other=other):
                c = color[4 * slot + side]
                out_ref[SOURCE + 4 * i + side] = c
                out_ref[MEET + c] = jnp.bitwise_xor(other, me)
                out_ref[SEND + c] = 4 * i + (side ^ 1)

                @pl.when(c >= ROUNDS)
                def _():
                    out_ref[LATE] = 1

            row_live = padding_ref[pl.ds(safe, 1), :].astype(jnp.float32)
            if side < 2:
                token = lax.broadcasted_iota(jnp.int32, (ROWS, STRIP), 0)
                place = lax.broadcasted_iota(jnp.int32, (ROWS, STRIP), 1)
                band = 2 * RIM
                wanted = lax.shift_right_logical(place, 3) * SIDE + jnp.bitwise_and(place, band - 1)
                wanted = wanted + (SIDE - band if side == 0 else 0)
                chosen = jnp.where(token == wanted, 1.0, 0.0)
                strip = jnp.dot(row_live, chosen, preferred_element_type=jnp.float32)
            else:
                strip = row_live[:, ROWS - STRIP :] if side == 2 else row_live[:, :STRIP]
            begin = ROWS + side * STRIP
            mask_ref[i : i + 1, begin : begin + STRIP] = jnp.where(has, strip, 0.0)

    core = jnp.bitwise_and(me, 1)
    chip = lax.shift_right_logical(me, 1)
    chips = count // 2
    order, _ = ring_pairs(count)
    plan_of_ring = ring_steps(chips, rows)
    out_ref[CORE] = core if len(plan_of_ring) > 1 else jnp.int32(0)
    for index, (step, cut) in enumerate(plan_of_ring):
        start = jnp.int32(0)
        if len(plan_of_ring) > 1:
            for rank, c in enumerate(order):
                start = jnp.where(chip == c, order[(rank + step) % chips] * rows + cut, start)
        out_ref[PLACE + index] = start


def ring_pairs(count):
    chips = count // 2
    order = list(range(0, chips, 2)) + list(range(chips - 1 - chips % 2, 0, -2))
    forward = []
    for index, chip in enumerate(order):
        after = order[(index + 1) % chips]
        forward += [(2 * chip + c, 2 * after + c) for c in range(2)]
    return order, forward


def ring_steps(chips, rows):
    if chips > 8:
        return [(0, 0)]
    pieces = [(0, 0)]
    for step in range(1, chips // 2 + 1):
        if 2 * step < chips:
            pieces += [(-step, 0), (step, 0)]
        else:
            pieces += [(-step, 0), (step, rows // 32 * 16)]
    return pieces


def route(plan, neighbours, position, padding, rows):
    count = plan.shape[0]
    smem = pl.BlockSpec(memory_space=pltpu.SMEM)
    vmem = pl.BlockSpec(memory_space=pltpu.VMEM)
    return pl.pallas_call(
        functools.partial(routing, count, rows),
        out_shape=(
            jax.ShapeDtypeStruct((64,), jnp.int32),
            jax.ShapeDtypeStruct((HOLD, KEYS), jnp.float32),
        ),
        in_specs=[smem] * 3 + [vmem],
        out_specs=(smem, vmem),
        scratch_shapes=[
            pltpu.SMEM((HOLD * count,), jnp.int32),
            pltpu.SMEM((count,), jnp.int32),
            pltpu.SMEM((4 * HOLD * count,), jnp.int32),
        ],
        name="routing",
    )(plan, neighbours.reshape(-1), position.reshape(1), padding)


def prepare_kernel(tokens_ref, gain_ref, info_ref, normed_ref, strips_ref):
    gain = gain_ref[...]
    band = 2 * RIM

    def normal(values):
        offset = values - jnp.mean(values, -1, keepdims=True)
        spread = jnp.mean(offset * offset, -1, keepdims=True)
        return offset * lax.rsqrt(spread + 1e-06) * gain

    for slot in range(HOLD):

        @pl.when(info_ref[LIVE + slot] == 1)
        def _(slot=slot):
            def pair(i, _):
                lines = []
                for half in range(2):
                    span = pl.ds(pl.multiple_of((2 * i + half) * SIDE, SIDE), SIDE)
                    line = normal(tokens_ref[slot, span, :].astype(jnp.float32))
                    normed_ref[slot, span, :] = line.astype(BF)
                    lines.append(line)
                span = pl.ds(pl.multiple_of(i * 2 * band, 2 * band), 2 * band)
                last = jnp.concatenate([line[SIDE - band :] for line in lines], 0)
                first = jnp.concatenate([line[:band] for line in lines], 0)
                strips_ref[4 * slot, span, :] = last.astype(BF)
                strips_ref[4 * slot + 1, span, :] = first.astype(BF)
                return 0

            lax.fori_loop(0, HALF // 2, pair, 0)
            strips_ref[4 * slot + 2] = normed_ref[slot, ROWS - STRIP :, :]
            strips_ref[4 * slot + 3] = normed_ref[slot, :STRIP, :]


def prepare(tokens, gain, info):
    width = tokens.shape[-1]
    vmem = pl.BlockSpec(memory_space=pltpu.VMEM)
    smem = pl.BlockSpec(memory_space=pltpu.SMEM)
    return pl.pallas_call(
        prepare_kernel,
        out_shape=(
            jax.ShapeDtypeStruct(tokens.shape, BF),
            jax.ShapeDtypeStruct((4 * HOLD, STRIP, width), BF),
        ),
        in_specs=[vmem, vmem, smem],
        out_specs=(vmem, vmem),
        compiler_params=pltpu.CompilerParams(vmem_limit_bytes=48 * 1024 * 1024),
        name="prepare",
    )(tokens, gain, info)


def branch_kernel(pieces, *refs):
    info_ref, mask_ref, normed_ref, strips_ref, late_ref = refs[:5]
    rims = refs[5 : 5 + ROUNDS]
    refs = refs[5 + ROUNDS :]
    mine, other = refs[:pieces], refs[pieces : 2 * pieces]
    out_ref = refs[2 * pieces]
    rows_in, weights, keys_all, queries, mixed, sems, row_sems = refs[2 * pieces + 1 :]
    core = info_ref[CORE]

    def weight_copies():
        for i in range(pieces):
            size = mine[i].shape[0]
            span = pl.ds(pl.multiple_of(info_ref[PLACE + i], 16), size)
            yield pltpu.make_async_copy(mine[i], weights.at[core, span, :], sems.at[0, i])
            yield pltpu.make_async_copy(other[i], weights.at[1 - core, span, :], sems.at[1, i])

    for slot in range(HOLD):

        @pl.when(info_ref[LIVE + slot] == 1)
        def _(slot=slot):
            target = rows_in.at[slot, pl.ds(0, ROWS), :]
            pltpu.make_async_copy(normed_ref.at[slot], target, row_sems.at[slot, 4]).start()
            for side in range(4):
                source = info_ref[SOURCE + 4 * slot + side]
                span = pl.ds(ROWS + side * STRIP, STRIP)
                target = rows_in.at[slot, span, :]
                sem = row_sems.at[slot, side]
                for r in range(ROUNDS):

                    @pl.when(source == r)
                    def _(r=r, target=target, sem=sem):
                        pltpu.make_async_copy(rims[r], target, sem).start()

                @pl.when((source >= ROUNDS) & (source < MOST))
                def _(source=source, target=target, sem=sem):
                    pltpu.make_async_copy(late_ref.at[source - ROUNDS], target, sem).start()

                @pl.when((source >= LOCAL) & (source < NONE))
                def _(source=source, target=target, sem=sem):
                    pltpu.make_async_copy(strips_ref.at[source - LOCAL], target, sem).start()

                @pl.when(source == NONE)
                def _(slot=slot, span=span):
                    rows_in[slot, span, :] = jnp.zeros((STRIP, rows_in.shape[2]), BF)

    for copy in weight_copies():
        copy.start()
    for copy in weight_copies():
        copy.wait()

    block = 256
    factor = math.log2(math.e) / math.sqrt(HS)
    dims = (((1,), (1,)), ((), ()))
    mixed[:, :LEAD] = jnp.zeros((ROWS, LEAD), BF)

    def work(slot, _):
        live = info_ref[LIVE + slot] == 1

        @pl.when(live)
        def _():
            target = rows_in.at[slot, pl.ds(0, ROWS), :]
            pltpu.make_async_copy(normed_ref.at[slot], target, row_sems.at[slot, 4]).wait()
            for side in range(4):

                @pl.when(info_ref[SOURCE + 4 * slot + side] != NONE)
                def _(side=side):
                    target = rows_in.at[slot, pl.ds(ROWS + side * STRIP, STRIP), :]
                    pltpu.make_async_copy(rims[0], target, row_sems.at[slot, side]).wait()

            def make_queries(i, _):
                span = pl.ds(pl.multiple_of(i * block, block), block)
                total = jnp.dot(
                    rows_in[slot, span, :], weights[1, :, :HW], preferred_element_type=jnp.float32
                )
                queries[span, :] = total.astype(BF)
                return 0

            lax.fori_loop(0, ROWS // block, make_queries, 0)

            def make_keys(i, _):
                span = pl.ds(pl.multiple_of(i * block, block), block)
                total = jnp.dot(
                    rows_in[slot, span, :], weights[0], preferred_element_type=jnp.float32
                )
                keys_all[span, :] = total.astype(BF)
                return 0

            lax.fori_loop(0, KEYS // block, make_keys, 0)
            usable = mask_ref[pl.ds(slot, 1), :] > 0.5
            for h in range(HEADS):
                span = slice(h * HS, (h + 1) * HS)
                scores = lax.dot_general(
                    queries[:, span], keys_all[:, span], dims, preferred_element_type=jnp.float32
                )
                scores = jnp.where(usable, scores * factor, -1e30)
                share = jnp.exp2(scores - jnp.max(scores, -1, keepdims=True))
                prob = (share * (1.0 / jnp.sum(share, -1, keepdims=True))).astype(BF)
                values = keys_all[:, HW + h * HS : HW + (h + 1) * HS]
                total = jnp.dot(prob, values, preferred_element_type=jnp.float32)
                mixed[:, LEAD + h * HS : LEAD + (h + 1) * HS] = total.astype(BF)

            def project(i, _):
                span = pl.ds(pl.multiple_of(i * block, block), block)
                total = lax.dot_general(
                    mixed[span, :],
                    weights[1, :, HW - LEAD :],
                    dims,
                    preferred_element_type=jnp.float32,
                )
                out_ref[slot, span, :] = total.astype(BF)
                return 0

            lax.fori_loop(0, ROWS // block, project, 0)

        @pl.when(jnp.logical_not(live))
        def _():
            out_ref[slot] = jnp.zeros(out_ref.shape[1:], BF)

        return 0

    lax.fori_loop(0, HOLD, work, 0)


def branch(info, mask, normed, strips, late, rims, mine, other):
    width = normed.shape[2]
    pieces = len(mine)
    anywhere = pl.BlockSpec(memory_space=pl.ANY)
    vmem = pl.BlockSpec(memory_space=pltpu.VMEM)
    smem = pl.BlockSpec(memory_space=pltpu.SMEM)
    return pl.pallas_call(
        functools.partial(branch_kernel, pieces),
        out_shape=jax.ShapeDtypeStruct(normed.shape, BF),
        in_specs=[smem, vmem] + [anywhere] * (3 + ROUNDS + 2 * pieces),
        out_specs=vmem,
        scratch_shapes=[
            pltpu.VMEM((HOLD, KEYS, width), BF),
            pltpu.VMEM((2, width, 2 * HW), BF),
            pltpu.VMEM((KEYS, 2 * HW), BF),
            pltpu.VMEM((ROWS, HW), BF),
            pltpu.VMEM((ROWS, LEAD + HW), BF),
            pltpu.SemaphoreType.DMA((2, pieces)),
            pltpu.SemaphoreType.DMA((HOLD, 5)),
        ],
        compiler_params=pltpu.CompilerParams(vmem_limit_bytes=60 * 1024 * 1024),
        name="branch",
    )(info, mask, normed, strips, late, *rims, *mine, *other)


def meet(choice, block, count, otherwise):
    def way(r):
        pairs = [(t, t ^ r) for t in range(count) if t ^ r < count]
        return lambda items: lax.ppermute(items[0], "tiles", pairs)

    ways = [lambda items: items[1]] + [way(r) for r in range(1, count)]
    return lax.switch(choice, ways, (block, otherwise))


def shards(tokens, padding, plan, neighbours, norm_gain, attention_weight, output_weight):
    count = lax.axis_size("tiles")
    chips = count // 2
    position = lax.axis_index("tiles")
    core = position % 2
    width = tokens.shape[2]
    rows = 2 * attention_weight.shape[0]
    info, mask = route(plan, neighbours, position, padding, rows)
    key_part = attention_weight[:, HW:]
    other_part = jnp.concatenate([attention_weight[:, :HW], output_weight.T], 1)
    nothing = jnp.zeros((STRIP, width), BF)
    normed, strips = prepare(tokens, norm_gain[None, :], info)

    def exchange(r):
        block = lax.dynamic_index_in_dim(strips, info[SEND + r], 0, keepdims=False)
        return meet(info[MEET + r], block, count, nothing)

    if chips > 8:
        rims = lax.map(exchange, jnp.arange(ROUNDS, dtype=jnp.int32))
        rims = [rims[r] for r in range(ROUNDS)]
        mine = [lax.all_gather(key_part, "tiles", axis=0, tiled=True)]
        other = [lax.all_gather(other_part, "tiles", axis=0, tiled=True)]
    else:
        order, forward = ring_pairs(count)
        backward = [(b, a) for a, b in forward]
        swap = [(t, t ^ 1) for t in range(count)]
        kept = jnp.where(core == 0, key_part, other_part)
        given = jnp.where(core == 0, other_part, key_part)
        peer = lax.ppermute(given, "tiles", swap)
        block = jnp.concatenate(
            [jnp.where(core == 0, kept, peer), jnp.where(core == 0, peer, kept)], 0
        )
        cut = rows // 32 * 16
        mine, other, rims = [block], [], []
        ahead = behind = block
        fresh = [block]
        last = chips // 2
        for step in range(1, last + 1):
            if 2 * step < chips:
                ahead = lax.ppermute(ahead, "tiles", forward)
                behind = lax.ppermute(behind, "tiles", backward)
            else:
                ahead = lax.ppermute(ahead[:cut], "tiles", forward)
                behind = lax.ppermute(behind[cut:], "tiles", backward)
            swapped = [lax.ppermute(piece, "tiles", swap) for piece in fresh]
            begin, end = ROUNDS * (step - 1) // last, ROUNDS * step // last
            met = [exchange(r) for r in range(begin, end)]
            (ahead, behind, strips), swapped, met = lax.optimization_barrier(
                ((ahead, behind, strips), swapped, met)
            )
            other += swapped
            rims += met
            fresh = [ahead, behind]
            mine += fresh
        other += [lax.ppermute(piece, "tiles", swap) for piece in fresh]

    late = lax.cond(
        info[LATE] == 1,
        lambda: lax.map(exchange, jnp.arange(ROUNDS, MOST, dtype=jnp.int32)),
        lambda: jnp.zeros((MOST - ROUNDS, STRIP, width), BF),
    )
    return branch(info, mask, normed, strips, late, rims, mine, other)


def solution(mesh):
    return jax.shard_map(
        shards,
        mesh=mesh,
        in_specs=(
            P(("groups", "tiles"), None, None),
            P("groups", None),
            P("groups"),
            P("groups", None),
            P(),
            P("tiles", None),
            P(None, "tiles"),
        ),
        out_specs=P(("groups", "tiles"), None, None),
        check_vma=False,
    )
```

```python
import functools
import math

import jax
import jax.numpy as jnp
from jax import lax
from jax.experimental import pallas as pl
from jax.experimental.pallas import tpu as pltpu
from jax.sharding import PartitionSpec as P

HEADS = 8
HS = 104
HW = HEADS * HS
SIDE = 32
HALF = 16
RIM = 4
ROWS = 512
STRIP = 128
KEYS = ROWS + 4 * STRIP
HOLD = 2
LANES = 128
LEAD = 64
BF = jnp.bfloat16

ROUNDS, MOST = 8, 15
NEAR = 0
MEET, SEND, SOURCE, LIVE, LATE, CORE, PLACE, GIVE = 0, 16, 32, 40, 42, 43, 44, 53
LOCAL, NONE, BESIDE = 16, 32, 40


def routing(count, rows, plan_ref, beside_ref, me_ref, padding_ref, out_ref, mask_ref, live, used, near, color, tally, edges):
    me = me_ref[0]
    slots = HOLD * count

    def clear(s, _):
        live[s] = 0
        return 0

    lax.fori_loop(0, slots, clear, 0)

    def mark(j, _):
        live[plan_ref[j]] = 1
        return 0

    lax.fori_loop(0, count, mark, 0)

    def empty(t, _):
        used[t] = 0
        near[t] = 0
        return 0

    lax.fori_loop(0, count, empty, 0)

    for weight in range(3):
        tally[weight] = 0

    def collect(e, _):
        s = lax.shift_right_logical(e, 1)
        side = 1 + 2 * jnp.bitwise_and(e, 1)
        n = beside_ref[4 * s + side]
        safe = jnp.maximum(n, 0)
        a, b = lax.shift_right_logical(s, 1), lax.shift_right_logical(safe, 1)

        @pl.when((n >= 0) & (a != b))
        def _():
            heavy = live[2 * a] * live[2 * a + 1] + live[2 * b] * live[2 * b + 1]
            place = tally[heavy]
            edges[2 * slots * heavy + place] = 4 * s + side
            tally[heavy] = place + 1

        return 0

    lax.fori_loop(0, 2 * slots, collect, 0)
    for weight in (2, 1, 0):

        def edge(e, _, weight=weight):
            key = edges[2 * slots * weight + e]
            s = lax.shift_right_logical(key, 2)
            side = jnp.bitwise_and(key, 3)
            n = beside_ref[key]
            a, b = lax.shift_right_logical(s, 1), lax.shift_right_logical(n, 1)
            apart = jnp.bitwise_xor(a, b)
            pair = jnp.bitwise_and(lax.shift_right_logical(near[a], jnp.minimum(apart, 31)), 1)
            close = (apart <= NEAR) & (pair == 0)
            mark_near = jnp.where(close, lax.shift_left(jnp.int32(1), jnp.minimum(apart, 31)), 0)
            near[a] = jnp.bitwise_or(near[a], mark_near)
            near[b] = jnp.bitwise_or(near[b], mark_near)
            taken = jnp.bitwise_or(used[a], used[b])
            first = lax.while_loop(
                lambda c: jnp.bitwise_and(lax.shift_right_logical(taken, c), 1) == 1,
                lambda c: c + 1,
                jnp.int32(0),
            )
            bit = jnp.where(close, 0, lax.shift_left(jnp.int32(1), first))
            first = jnp.where(close, BESIDE + apart, first)
            used[a] = jnp.bitwise_or(used[a], bit)
            used[b] = jnp.bitwise_or(used[b], bit)
            color[key] = first
            color[4 * n + jnp.bitwise_xor(side, 1)] = first
            return 0

        lax.fori_loop(0, tally[weight], edge, 0)

    for r in range(MOST + 1):
        out_ref[MEET + r] = 0
        out_ref[SEND + r] = 0
    out_ref[LATE] = 0
    for r in range(NEAR + 1):
        out_ref[GIVE + r] = 0
    for i in range(HOLD):
        slot = HOLD * me + i
        out_ref[LIVE + i] = live[slot]
        mask_ref[i : i + 1, :ROWS] = padding_ref[pl.ds(slot, 1), :].astype(jnp.float32)
        for side in range(4):
            n = beside_ref[4 * slot + side]
            has = (n >= 0) & (live[slot] == 1)
            safe = jnp.maximum(n, 0)
            other = lax.shift_right_logical(safe, 1)
            away = has & (other != me)
            out_ref[SOURCE + 4 * i + side] = jnp.where(has, LOCAL + 4 * jnp.bitwise_and(safe, 1) + side, NONE)

            @pl.when(away)
            def _(i=i, side=side, slot=slot, other=other):
                c = color[4 * slot + side]
                out_ref[SOURCE + 4 * i + side] = c

                @pl.when(c >= BESIDE)
                def _():
                    out_ref[GIVE + c - BESIDE] = 4 * i + (side ^ 1)

                @pl.when(c < BESIDE)
                def _():
                    out_ref[MEET + c] = jnp.bitwise_xor(other, me)
                    out_ref[SEND + c] = 4 * i + (side ^ 1)

                @pl.when((c >= ROUNDS) & (c < BESIDE))
                def _():
                    out_ref[LATE] = 1

            row_live = padding_ref[pl.ds(safe, 1), :].astype(jnp.float32)
            if side < 2:
                token = lax.broadcasted_iota(jnp.int32, (ROWS, STRIP), 0)
                place = lax.broadcasted_iota(jnp.int32, (ROWS, STRIP), 1)
                band = 2 * RIM
                wanted = lax.shift_right_logical(place, 3) * SIDE + jnp.bitwise_and(place, band - 1)
                wanted = wanted + (SIDE - band if side == 0 else 0)
                chosen = jnp.where(token == wanted, 1.0, 0.0).astype(BF)
                strip = jnp.dot(row_live.astype(BF), chosen, preferred_element_type=jnp.float32)
            else:
                strip = row_live[:, ROWS - STRIP :] if side == 2 else row_live[:, :STRIP]
            begin = ROWS + side * STRIP
            mask_ref[i : i + 1, begin : begin + STRIP] = jnp.where(has, strip, 0.0)

    core = jnp.bitwise_and(me, 1)
    chip = lax.shift_right_logical(me, 1)
    chips = count // 2
    order, _ = ring_pairs(count)
    plan_of_ring = ring_steps(chips, rows)
    out_ref[CORE] = core if len(plan_of_ring) > 1 else jnp.int32(0)
    for index, (step, cut) in enumerate(plan_of_ring):
        start = jnp.int32(0)
        if len(plan_of_ring) > 1:
            for rank, c in enumerate(order):
                start = jnp.where(chip == c, order[(rank + step) % chips] * rows + cut, start)
        out_ref[PLACE + index] = start


def ring_pairs(count):
    chips = count // 2
    order = list(range(0, chips, 2)) + list(range(chips - 1 - chips % 2, 0, -2))
    forward = []
    for index, chip in enumerate(order):
        after = order[(index + 1) % chips]
        forward += [(2 * chip + c, 2 * after + c) for c in range(2)]
    return order, forward


def ring_steps(chips, rows):
    if chips > 8:
        return [(0, 0)]
    pieces = [(0, 0)]
    for step in range(1, chips // 2 + 1):
        if 2 * step < chips:
            pieces += [(-step, 0), (step, 0)]
        else:
            pieces += [(-step, 0), (step, rows // 32 * 16)]
    return pieces


def route(plan, neighbours, position, padding, rows):
    count = plan.shape[0]
    smem = pl.BlockSpec(memory_space=pltpu.SMEM)
    vmem = pl.BlockSpec(memory_space=pltpu.VMEM)
    return pl.pallas_call(
        functools.partial(routing, count, rows),
        out_shape=(
            jax.ShapeDtypeStruct((64,), jnp.int32),
            jax.ShapeDtypeStruct((HOLD, KEYS), jnp.float32),
        ),
        in_specs=[smem] * 3 + [vmem],
        out_specs=(smem, vmem),
        scratch_shapes=[
            pltpu.SMEM((HOLD * count,), jnp.int32),
            pltpu.SMEM((count,), jnp.int32),
            pltpu.SMEM((count,), jnp.int32),
            pltpu.SMEM((4 * HOLD * count,), jnp.int32),
            pltpu.SMEM((3,), jnp.int32),
            pltpu.SMEM((6 * HOLD * count,), jnp.int32),
        ],
        name="routing",
    )(plan, neighbours.reshape(-1), position.reshape(1), padding)


def prepare_kernel(tokens_ref, gain_ref, info_ref, normed_ref, strips_ref, *sends):
    gain = gain_ref[...]
    band = 2 * RIM

    def normal(values):
        offset = values - jnp.mean(values, -1, keepdims=True)
        spread = jnp.mean(offset * offset, -1, keepdims=True)
        return offset * lax.rsqrt(spread + 1e-06) * gain

    for slot in range(HOLD):

        @pl.when(info_ref[LIVE + slot] == 1)
        def _(slot=slot):
            def pair(i, _):
                lines = []
                for half in range(2):
                    span = pl.ds(pl.multiple_of((2 * i + half) * SIDE, SIDE), SIDE)
                    line = normal(tokens_ref[slot, span, :].astype(jnp.float32))
                    normed_ref[slot, span, :] = line.astype(BF)
                    lines.append(line)
                span = pl.ds(pl.multiple_of(i * 2 * band, 2 * band), 2 * band)
                last = jnp.concatenate([line[SIDE - band :] for line in lines], 0)
                first = jnp.concatenate([line[:band] for line in lines], 0)
                strips_ref[4 * slot, span, :] = last.astype(BF)
                strips_ref[4 * slot + 1, span, :] = first.astype(BF)
                return 0

            lax.fori_loop(0, HALF // 2, pair, 0)
            strips_ref[4 * slot + 2] = normed_ref[slot, ROWS - STRIP :, :]
            strips_ref[4 * slot + 3] = normed_ref[slot, :STRIP, :]

    for r in range(1, NEAR + 1):
        sends[r - 1][...] = strips_ref[info_ref[GIVE + r]]
    for r in range(ROUNDS):

        @pl.when(info_ref[MEET + r] != 0)
        def _(r=r):
            sends[NEAR + r][...] = strips_ref[info_ref[SEND + r]]


def prepare(tokens, gain, info):
    width = tokens.shape[-1]
    vmem = pl.BlockSpec(memory_space=pltpu.VMEM)
    smem = pl.BlockSpec(memory_space=pltpu.SMEM)
    return pl.pallas_call(
        prepare_kernel,
        out_shape=(
            jax.ShapeDtypeStruct(tokens.shape, BF),
            jax.ShapeDtypeStruct((4 * HOLD, STRIP, width), BF),
        )
        + (jax.ShapeDtypeStruct((STRIP, width), BF),) * (NEAR + ROUNDS),
        in_specs=[vmem, vmem, smem],
        out_specs=(vmem,) * (2 + NEAR + ROUNDS),
        compiler_params=pltpu.CompilerParams(vmem_limit_bytes=48 * 1024 * 1024),
        name="prepare",
    )(tokens, gain, info)


def branch_kernel(pieces, *refs):
    info_ref, mask_ref, normed_ref, strips_ref, late_ref = refs[:5]
    rims = refs[5 : 5 + ROUNDS]
    close = refs[5 + ROUNDS : 5 + ROUNDS + NEAR]
    refs = refs[5 + ROUNDS + NEAR :]
    mine, other = refs[:pieces], refs[pieces : 2 * pieces]
    out_ref = refs[2 * pieces]
    rows_in, weights, keys, values, queries, mixed, sems, row_sems = refs[2 * pieces + 1 :]
    core = info_ref[CORE]

    def weight_copies():
        for i in range(pieces):
            size = mine[i].shape[0]
            span = pl.ds(pl.multiple_of(info_ref[PLACE + i], 16), size)
            yield pltpu.make_async_copy(mine[i], weights.at[core, span, :], sems.at[0, i])
            yield pltpu.make_async_copy(other[i], weights.at[1 - core, span, :], sems.at[1, i])

    for slot in range(HOLD):

        @pl.when(info_ref[LIVE + slot] == 1)
        def _(slot=slot):
            target = rows_in.at[slot, pl.ds(0, ROWS), :]
            pltpu.make_async_copy(normed_ref.at[slot], target, row_sems.at[slot, 4]).start()
            for side in range(4):
                source = info_ref[SOURCE + 4 * slot + side]
                span = pl.ds(ROWS + side * STRIP, STRIP)
                target = rows_in.at[slot, span, :]
                sem = row_sems.at[slot, side]
                for r in range(ROUNDS):

                    @pl.when(source == r)
                    def _(r=r, target=target, sem=sem):
                        pltpu.make_async_copy(rims[r], target, sem).start()

                for r in range(1, NEAR + 1):

                    @pl.when(source == BESIDE + r)
                    def _(r=r, target=target, sem=sem):
                        pltpu.make_async_copy(close[r - 1], target, sem).start()

                @pl.when((source >= ROUNDS) & (source < MOST))
                def _(source=source, target=target, sem=sem):
                    pltpu.make_async_copy(late_ref.at[source - ROUNDS], target, sem).start()

                @pl.when((source >= LOCAL) & (source < NONE))
                def _(source=source, target=target, sem=sem):
                    pltpu.make_async_copy(strips_ref.at[source - LOCAL], target, sem).start()

                @pl.when(source == NONE)
                def _(slot=slot, span=span):
                    rows_in[slot, span, :] = jnp.zeros((STRIP, rows_in.shape[2]), BF)

    for copy in weight_copies():
        copy.start()
    for copy in weight_copies():
        copy.wait()

    block = 256
    factor = math.log2(math.e) / math.sqrt(HS)
    dims = (((1,), (1,)), ((), ()))
    mixed[:, :LEAD] = jnp.zeros((ROWS, LEAD), BF)
    lane = lax.broadcasted_iota(jnp.int32, (KEYS, LANES), 1)
    one = jnp.where(lane == HS, 1.0, 0.0).astype(BF)
    for h in range(HEADS):
        queries[h] = one[:ROWS]
        values[h] = one

    def work(slot, _):
        live = info_ref[LIVE + slot] == 1

        @pl.when(live)
        def _():
            away = jnp.where(mask_ref[pl.ds(slot, 1), :] > 0.5, 0.0, -1e30)
            away = jnp.broadcast_to(away, (LANES, KEYS)).T
            away = jnp.where(lane == HS, away, 0.0).astype(BF)
            for h in range(HEADS):
                keys[h] = away
            target = rows_in.at[slot, pl.ds(0, ROWS), :]
            pltpu.make_async_copy(normed_ref.at[slot], target, row_sems.at[slot, 4]).wait()
            for side in range(4):

                @pl.when(info_ref[SOURCE + 4 * slot + side] != NONE)
                def _(side=side):
                    target = rows_in.at[slot, pl.ds(ROWS + side * STRIP, STRIP), :]
                    pltpu.make_async_copy(rims[0], target, row_sems.at[slot, side]).wait()

            def make_queries(i, _):
                span = pl.ds(pl.multiple_of(i * block, block), block)
                total = jnp.dot(
                    rows_in[slot, span, :], weights[1, :, :HW], preferred_element_type=jnp.float32
                ).astype(BF)
                for h in range(HEADS):
                    queries[h, span, :HS] = total[:, h * HS : (h + 1) * HS]
                return 0

            lax.fori_loop(0, ROWS // block, make_queries, 0)

            def make_keys(i, _):
                span = pl.ds(pl.multiple_of(i * block, block), block)
                total = jnp.dot(
                    rows_in[slot, span, :], weights[0], preferred_element_type=jnp.float32
                ).astype(BF)
                for h in range(HEADS):
                    keys[h, span, :HS] = total[:, h * HS : (h + 1) * HS]
                    values[h, span, :HS] = total[:, HW + h * HS : HW + (h + 1) * HS]
                return 0

            lax.fori_loop(0, KEYS // block, make_keys, 0)
            for h in range(HEADS):
                scores = lax.dot_general(
                    queries[h], keys[h], dims, preferred_element_type=jnp.float32
                )
                highest = jnp.max(scores, -1, keepdims=True)
                share = jnp.exp2((scores - highest) * factor).astype(BF)
                total = jnp.dot(share, values[h], preferred_element_type=jnp.float32)
                total = total[:, :HS] * (1.0 / total[:, HS : HS + 1])
                mixed[:, LEAD + h * HS : LEAD + (h + 1) * HS] = total.astype(BF)

            def project(i, _):
                span = pl.ds(pl.multiple_of(i * block, block), block)
                total = lax.dot_general(
                    mixed[span, :],
                    weights[1, :, HW - LEAD :],
                    dims,
                    preferred_element_type=jnp.float32,
                )
                out_ref[slot, span, :] = total.astype(BF)
                return 0

            lax.fori_loop(0, ROWS // block, project, 0)

        @pl.when(jnp.logical_not(live))
        def _():
            out_ref[slot] = jnp.zeros(out_ref.shape[1:], BF)

        return 0

    lax.fori_loop(0, HOLD, work, 0)


def branch(info, mask, normed, strips, late, rims, close, mine, other):
    width = normed.shape[2]
    pieces = len(mine)
    anywhere = pl.BlockSpec(memory_space=pl.ANY)
    vmem = pl.BlockSpec(memory_space=pltpu.VMEM)
    smem = pl.BlockSpec(memory_space=pltpu.SMEM)
    return pl.pallas_call(
        functools.partial(branch_kernel, pieces),
        out_shape=jax.ShapeDtypeStruct(normed.shape, BF),
        in_specs=[smem, vmem] + [anywhere] * (3 + ROUNDS + NEAR + 2 * pieces),
        out_specs=vmem,
        scratch_shapes=[
            pltpu.VMEM((HOLD, KEYS, width), BF),
            pltpu.VMEM((2, width, 2 * HW), BF),
            pltpu.VMEM((HEADS, KEYS, LANES), BF),
            pltpu.VMEM((HEADS, KEYS, LANES), BF),
            pltpu.VMEM((HEADS, ROWS, LANES), BF),
            pltpu.VMEM((ROWS, LEAD + HW), BF),
            pltpu.SemaphoreType.DMA((2, pieces)),
            pltpu.SemaphoreType.DMA((HOLD, 5)),
        ],
        compiler_params=pltpu.CompilerParams(vmem_limit_bytes=60 * 1024 * 1024),
        name="branch",
    )(info, mask, normed, strips, late, *rims, *close, *mine, *other)


def meet(choice, block, count, otherwise):
    def way(r):
        pairs = [(t, t ^ r) for t in range(count) if t ^ r < count]
        return lambda items: lax.ppermute(items[0], "tiles", pairs)

    ways = [lambda items: items[1]] + [way(r) for r in range(1, count)]
    return lax.switch(choice, ways, (block, otherwise))


def shards(tokens, padding, plan, neighbours, norm_gain, attention_weight, output_weight):
    count = lax.axis_size("tiles")
    chips = count // 2
    position = lax.axis_index("tiles")
    core = position % 2
    width = tokens.shape[2]
    rows = 2 * attention_weight.shape[0]
    info, mask = route(plan, neighbours, position, padding, rows)
    key_part = attention_weight[:, HW:]
    other_part = jnp.concatenate([attention_weight[:, :HW], output_weight.T], 1)
    nothing = jnp.zeros((STRIP, width), BF)

    def exchange(r, strips):
        block = lax.dynamic_index_in_dim(strips, info[SEND + r], 0, keepdims=False)
        return meet(info[MEET + r], block, count, nothing)

    def meet_round(r, sends):
        return meet(info[MEET + r], sends[NEAR + r], count, nothing)

    def give(sends):
        result = []
        for r in range(1, NEAR + 1):
            pairs = [(t, t ^ r) for t in range(count) if t ^ r < count]
            result.append(lax.ppermute(sends[r - 1], "tiles", pairs))
        return result

    if chips > 8:
        normed, strips, *sends = prepare(tokens, norm_gain[None, :], info)
        close = give(sends)
        rims = lax.map(lambda r: exchange(r, strips), jnp.arange(ROUNDS, dtype=jnp.int32))
        rims = [rims[r] for r in range(ROUNDS)]
        mine = [lax.all_gather(key_part, "tiles", axis=0, tiled=True)]
        other = [lax.all_gather(other_part, "tiles", axis=0, tiled=True)]
    else:
        order, forward = ring_pairs(count)
        backward = [(b, a) for a, b in forward]
        swap = [(t, t ^ 1) for t in range(count)]
        kept = jnp.where(core == 0, key_part, other_part)
        given = jnp.where(core == 0, other_part, key_part)
        peer = lax.ppermute(given, "tiles", swap)
        block = jnp.concatenate(
            [jnp.where(core == 0, kept, peer), jnp.where(core == 0, peer, kept)], 0
        )
        cut = rows // 32 * 16
        mine, other, rims = [block], [], []
        ahead = behind = block
        fresh = [block]
        last = chips // 2
        for step in range(1, last + 1):
            if 2 * step < chips:
                ahead = lax.ppermute(ahead, "tiles", forward)
                behind = lax.ppermute(behind, "tiles", backward)
            else:
                ahead = lax.ppermute(ahead[:cut], "tiles", forward)
                behind = lax.ppermute(behind[cut:], "tiles", backward)
            swapped = [lax.ppermute(piece, "tiles", swap) for piece in fresh]
            met = []
            if step == 1:
                normed, strips, *sends = prepare(tokens, norm_gain[None, :], info)
            elif step - 2 < ROUNDS:
                met = [meet_round(step - 2, sends)]
            (ahead, behind, sends), swapped, met = lax.optimization_barrier(
                ((ahead, behind, sends), swapped, met)
            )
            if step == 1:
                close = give(sends)
            other += swapped
            rims += met
            fresh = [ahead, behind]
            mine += fresh
        other += [lax.ppermute(piece, "tiles", swap) for piece in fresh]
        rims += [meet_round(r, sends) for r in range(len(rims), ROUNDS)]

    late = lax.cond(
        info[LATE] == 1,
        lambda: lax.map(lambda r: exchange(r, strips), jnp.arange(ROUNDS, MOST, dtype=jnp.int32)),
        lambda: jnp.zeros((MOST - ROUNDS, STRIP, width), BF),
    )
    return branch(info, mask, normed, strips, late, rims, close, mine, other)


def solution(mesh):
    return jax.shard_map(
        shards,
        mesh=mesh,
        in_specs=(
            P(("groups", "tiles"), None, None),
            P("groups", None),
            P("groups"),
            P("groups", None),
            P(),
            P("tiles", None),
            P(None, "tiles"),
        ),
        out_specs=P(("groups", "tiles"), None, None),
        check_vma=False,
    )
```

```python
import functools
import math

import jax
import jax.numpy as jnp
from jax import lax
from jax.experimental import pallas as pl
from jax.experimental.pallas import tpu as pltpu
from jax.sharding import PartitionSpec as P

HEADS = 8
HS = 104
HW = HEADS * HS
SIDE = 32
HALF = 16
RIM = 4
ROWS = 512
STRIP = 128
KEYS = ROWS + 4 * STRIP
HOLD = 2
LANES = 128
LEAD = 64
BF = jnp.bfloat16
PART = (2 * HW // LANES + 1) // 2 * LANES
REST = 2 * HW - PART

ROUNDS, MOST = 8, 15
NEAR = 0
MEET, SEND, SOURCE, LIVE, LATE, CORE, PLACE, GIVE, GROUP = 0, 16, 32, 40, 42, 43, 44, 53, 52
LOCAL, NONE, BESIDE = 16, 32, 40


def routing(count, rows, plan_ref, beside_ref, me_ref, padding_ref, out_ref, mask_ref, live, used, near, color, tally, edges):
    me = me_ref[0]
    slots = HOLD * count

    def clear(s, _):
        live[s] = 0
        return 0

    lax.fori_loop(0, slots, clear, 0)

    def mark(j, _):
        live[plan_ref[j]] = 1
        return 0

    lax.fori_loop(0, count, mark, 0)

    def empty(t, _):
        used[t] = 0
        near[t] = 0
        return 0

    lax.fori_loop(0, count, empty, 0)

    for weight in range(3):
        tally[weight] = 0

    def collect(e, _):
        s = lax.shift_right_logical(e, 1)
        side = 1 + 2 * jnp.bitwise_and(e, 1)
        n = beside_ref[4 * s + side]
        safe = jnp.maximum(n, 0)
        a, b = lax.shift_right_logical(s, 1), lax.shift_right_logical(safe, 1)

        @pl.when((n >= 0) & (a != b))
        def _():
            heavy = live[2 * a] * live[2 * a + 1] + live[2 * b] * live[2 * b + 1]
            place = tally[heavy]
            edges[2 * slots * heavy + place] = 4 * s + side
            tally[heavy] = place + 1

        return 0

    lax.fori_loop(0, 2 * slots, collect, 0)
    for weight in (2, 1, 0):

        def edge(e, _, weight=weight):
            key = edges[2 * slots * weight + e]
            s = lax.shift_right_logical(key, 2)
            side = jnp.bitwise_and(key, 3)
            n = beside_ref[key]
            a, b = lax.shift_right_logical(s, 1), lax.shift_right_logical(n, 1)
            apart = jnp.bitwise_xor(a, b)
            pair = jnp.bitwise_and(lax.shift_right_logical(near[a], jnp.minimum(apart, 31)), 1)
            close = (apart <= NEAR) & (pair == 0)
            mark_near = jnp.where(close, lax.shift_left(jnp.int32(1), jnp.minimum(apart, 31)), 0)
            near[a] = jnp.bitwise_or(near[a], mark_near)
            near[b] = jnp.bitwise_or(near[b], mark_near)
            taken = jnp.bitwise_or(used[a], used[b])
            first = lax.while_loop(
                lambda c: jnp.bitwise_and(lax.shift_right_logical(taken, c), 1) == 1,
                lambda c: c + 1,
                jnp.int32(0),
            )
            bit = jnp.where(close, 0, lax.shift_left(jnp.int32(1), first))
            first = jnp.where(close, BESIDE + apart, first)
            used[a] = jnp.bitwise_or(used[a], bit)
            used[b] = jnp.bitwise_or(used[b], bit)
            color[key] = first
            color[4 * n + jnp.bitwise_xor(side, 1)] = first
            return 0

        lax.fori_loop(0, tally[weight], edge, 0)

    for r in range(MOST + 1):
        out_ref[MEET + r] = 0
        out_ref[SEND + r] = 0
    out_ref[LATE] = 0
    for r in range(NEAR + 1):
        out_ref[GIVE + r] = 0
    for i in range(HOLD):
        slot = HOLD * me + i
        out_ref[LIVE + i] = live[slot]
        mask_ref[i : i + 1, :ROWS] = padding_ref[pl.ds(slot, 1), :].astype(jnp.float32)
        for side in range(4):
            n = beside_ref[4 * slot + side]
            has = (n >= 0) & (live[slot] == 1)
            safe = jnp.maximum(n, 0)
            other = lax.shift_right_logical(safe, 1)
            away = has & (other != me)
            out_ref[SOURCE + 4 * i + side] = jnp.where(has, LOCAL + 4 * jnp.bitwise_and(safe, 1) + side, NONE)

            @pl.when(away)
            def _(i=i, side=side, slot=slot, other=other):
                c = color[4 * slot + side]
                out_ref[SOURCE + 4 * i + side] = c

                @pl.when(c >= BESIDE)
                def _():
                    out_ref[GIVE + c - BESIDE] = 4 * i + (side ^ 1)

                @pl.when(c < BESIDE)
                def _():
                    out_ref[MEET + c] = jnp.bitwise_xor(other, me)
                    out_ref[SEND + c] = 4 * i + (side ^ 1)

                @pl.when((c >= ROUNDS) & (c < BESIDE))
                def _():
                    out_ref[LATE] = 1

            row_live = padding_ref[pl.ds(safe, 1), :].astype(jnp.float32)
            if side < 2:
                token = lax.broadcasted_iota(jnp.int32, (ROWS, STRIP), 0)
                place = lax.broadcasted_iota(jnp.int32, (ROWS, STRIP), 1)
                band = 2 * RIM
                wanted = lax.shift_right_logical(place, 3) * SIDE + jnp.bitwise_and(place, band - 1)
                wanted = wanted + (SIDE - band if side == 0 else 0)
                chosen = jnp.where(token == wanted, 1.0, 0.0).astype(BF)
                strip = jnp.dot(row_live.astype(BF), chosen, preferred_element_type=jnp.float32)
            else:
                strip = row_live[:, ROWS - STRIP :] if side == 2 else row_live[:, :STRIP]
            begin = ROWS + side * STRIP
            mask_ref[i : i + 1, begin : begin + STRIP] = jnp.where(has, strip, 0.0)

    core = jnp.bitwise_and(me, 1)
    chip = lax.shift_right_logical(me, 1)
    chips = count // 2
    order, _ = ring_pairs(count)
    plan_of_ring = ring_steps(chips)
    out_ref[CORE] = core if len(plan_of_ring) > 1 else jnp.int32(0)
    out_ref[GROUP] = me_ref[1]
    for index, step in enumerate(plan_of_ring):
        start = jnp.int32(0)
        if len(plan_of_ring) > 1:
            for rank, c in enumerate(order):
                start = jnp.where(chip == c, order[(rank + step) % chips] * rows, start)
        out_ref[PLACE + index] = start


def ring_pairs(count):
    chips = count // 2
    order = list(range(0, chips, 2)) + list(range(chips - 1 - chips % 2, 0, -2))
    forward = []
    for index, chip in enumerate(order):
        after = order[(index + 1) % chips]
        forward += [(2 * chip + c, 2 * after + c) for c in range(2)]
    return order, forward


def ring_steps(chips):
    if chips > 8:
        return [0]
    pieces = [0]
    for step in range(1, chips // 2 + 1):
        pieces += [-step, step] if 2 * step < chips else [-step]
    return pieces


def route(plan, neighbours, position, padding, rows):
    count = plan.shape[0]
    smem = pl.BlockSpec(memory_space=pltpu.SMEM)
    vmem = pl.BlockSpec(memory_space=pltpu.VMEM)
    return pl.pallas_call(
        functools.partial(routing, count, rows),
        out_shape=(
            jax.ShapeDtypeStruct((64,), jnp.int32),
            jax.ShapeDtypeStruct((HOLD, KEYS), jnp.float32),
        ),
        in_specs=[smem] * 3 + [vmem],
        out_specs=(smem, vmem),
        scratch_shapes=[
            pltpu.SMEM((HOLD * count,), jnp.int32),
            pltpu.SMEM((count,), jnp.int32),
            pltpu.SMEM((count,), jnp.int32),
            pltpu.SMEM((4 * HOLD * count,), jnp.int32),
            pltpu.SMEM((3,), jnp.int32),
            pltpu.SMEM((6 * HOLD * count,), jnp.int32),
        ],
        name="routing",
    )(plan, neighbours.reshape(-1), jnp.stack([position, lax.axis_index("groups")]), padding)


def prepare_kernel(tokens_ref, gain_ref, info_ref, normed_ref, strips_ref, *sends):
    gain = gain_ref[...]
    band = 2 * RIM

    def normal(values):
        offset = values - jnp.mean(values, -1, keepdims=True)
        spread = jnp.mean(offset * offset, -1, keepdims=True)
        return offset * lax.rsqrt(spread + 1e-06) * gain

    for slot in range(HOLD):

        @pl.when(info_ref[LIVE + slot] == 1)
        def _(slot=slot):
            def pair(i, _):
                lines = []
                for half in range(2):
                    span = pl.ds(pl.multiple_of((2 * i + half) * SIDE, SIDE), SIDE)
                    line = normal(tokens_ref[slot, span, :].astype(jnp.float32))
                    normed_ref[slot, span, :] = line.astype(BF)
                    lines.append(line)
                span = pl.ds(pl.multiple_of(i * 2 * band, 2 * band), 2 * band)
                last = jnp.concatenate([line[SIDE - band :] for line in lines], 0)
                first = jnp.concatenate([line[:band] for line in lines], 0)
                strips_ref[4 * slot, span, :] = last.astype(BF)
                strips_ref[4 * slot + 1, span, :] = first.astype(BF)
                return 0

            lax.fori_loop(0, HALF // 2, pair, 0)
            strips_ref[4 * slot + 2] = normed_ref[slot, ROWS - STRIP :, :]
            strips_ref[4 * slot + 3] = normed_ref[slot, :STRIP, :]

    for r in range(1, NEAR + 1):
        sends[r - 1][...] = strips_ref[info_ref[GIVE + r]]
    for r in range(ROUNDS):

        @pl.when(info_ref[MEET + r] != 0)
        def _(r=r):
            sends[NEAR + r][...] = strips_ref[info_ref[SEND + r]]


def prepare(tokens, gain, info):
    width = tokens.shape[-1]
    vmem = pl.BlockSpec(memory_space=pltpu.VMEM)
    smem = pl.BlockSpec(memory_space=pltpu.SMEM)
    return pl.pallas_call(
        prepare_kernel,
        out_shape=(
            jax.ShapeDtypeStruct(tokens.shape, BF),
            jax.ShapeDtypeStruct((4 * HOLD, STRIP, width), BF),
        )
        + (jax.ShapeDtypeStruct((STRIP, width), BF),) * (NEAR + ROUNDS),
        in_specs=[vmem, vmem, smem],
        out_specs=(vmem,) * (2 + NEAR + ROUNDS),
        compiler_params=pltpu.CompilerParams(vmem_limit_bytes=48 * 1024 * 1024),
        name="prepare",
    )(tokens, gain, info)


def branch_kernel(pieces, *refs):
    info_ref, mask_ref, normed_ref, strips_ref, late_ref = refs[:5]
    rims = refs[5 : 5 + ROUNDS]
    close = refs[5 + ROUNDS : 5 + ROUNDS + NEAR]
    refs = refs[5 + ROUNDS + NEAR :]
    mine, other = refs[:pieces], refs[pieces : 2 * pieces]
    refs = refs[2 * pieces :]
    far, far_other = refs[: pieces - 1], refs[pieces - 1 : 2 * pieces - 2]
    out_ref, rows_in, weights, keys, values, queries, mixed, sems, row_sems = refs[2 * pieces - 2 :]
    core, group = info_ref[CORE], info_ref[GROUP]

    def weight_copies(half, near, beyond):
        for i in range(pieces):
            target = weights.at[half, pl.ds(pl.multiple_of(info_ref[PLACE + i], 16), near[i].shape[0])]
            if i == 0:
                yield pltpu.make_async_copy(near[0], target, sems.at[half, 0])
                continue
            start = pl.multiple_of(group * REST, LANES)
            part = target.at[:, pl.ds(start, PART)]
            yield pltpu.make_async_copy(near[i], part, sems.at[half, 2 * i])
            first = pl.multiple_of((1 - group) * (PART - REST), LANES)
            source = beyond[i - 1].at[:, pl.ds(first, REST)]
            rest = target.at[:, pl.ds(pl.multiple_of((1 - group) * PART, LANES), REST)]
            yield pltpu.make_async_copy(source, rest, sems.at[half, 2 * i - 1])

    def start_weights(half):
        @pl.when(core == half)
        def _():
            for copy in weight_copies(half, mine, far):
                copy.start()

        @pl.when(core != half)
        def _():
            for copy in weight_copies(half, other, far_other):
                copy.start()

    for slot in range(HOLD):

        @pl.when(info_ref[LIVE + slot] == 1)
        def _(slot=slot):
            target = rows_in.at[slot, pl.ds(0, ROWS), :]
            pltpu.make_async_copy(normed_ref.at[slot], target, row_sems.at[slot, 4]).start()

    busy = info_ref[LIVE] + info_ref[LIVE + 1] > 0

    @pl.when(busy)
    def _():
        start_weights(1)
        start_weights(0)

    for slot in range(HOLD):

        @pl.when(info_ref[LIVE + slot] == 1)
        def _(slot=slot):
            for side in range(4):
                source = info_ref[SOURCE + 4 * slot + side]
                span = pl.ds(ROWS + side * STRIP, STRIP)
                target = rows_in.at[slot, span, :]
                sem = row_sems.at[slot, side]
                for r in range(ROUNDS):

                    @pl.when(source == r)
                    def _(r=r, target=target, sem=sem):
                        pltpu.make_async_copy(rims[r], target, sem).start()

                for r in range(1, NEAR + 1):

                    @pl.when(source == BESIDE + r)
                    def _(r=r, target=target, sem=sem):
                        pltpu.make_async_copy(close[r - 1], target, sem).start()

                @pl.when((source >= ROUNDS) & (source < MOST))
                def _(source=source, target=target, sem=sem):
                    pltpu.make_async_copy(late_ref.at[source - ROUNDS], target, sem).start()

                @pl.when((source >= LOCAL) & (source < NONE))
                def _(source=source, target=target, sem=sem):
                    pltpu.make_async_copy(strips_ref.at[source - LOCAL], target, sem).start()

                @pl.when(source == NONE)
                def _(slot=slot, span=span):
                    rows_in[slot, span, :] = jnp.zeros((STRIP, rows_in.shape[2]), BF)

    block = 256
    factor = math.log2(math.e) / math.sqrt(HS)
    dims = (((1,), (1,)), ((), ()))
    mixed[:, :LEAD] = jnp.zeros((ROWS, LEAD), BF)
    lane = lax.broadcasted_iota(jnp.int32, (KEYS, LANES), 1)
    one = jnp.where(lane == HS, 1.0, 0.0).astype(BF)
    for h in range(HEADS):
        queries[h] = one[:ROWS]
        values[h] = one

    def work(slot, _):
        live = info_ref[LIVE + slot] == 1

        @pl.when(live)
        def _():
            away = jnp.where(mask_ref[pl.ds(slot, 1), :] > 0.5, 0.0, -1e30)
            away = jnp.broadcast_to(away, (LANES, KEYS)).T
            away = jnp.where(lane == HS, away, 0.0).astype(BF)
            for h in range(HEADS):
                keys[h] = away
            initial = (slot == 0) | (info_ref[LIVE] == 0)

            def wait_weights(half):
                @pl.when(initial)
                def _():
                    for copy in weight_copies(half, mine, far):
                        copy.wait()

            target = rows_in.at[slot, pl.ds(0, ROWS), :]
            pltpu.make_async_copy(normed_ref.at[slot], target, row_sems.at[slot, 4]).wait()
            wait_weights(1)

            def make_queries(i, _):
                span = pl.ds(pl.multiple_of(i * block, block), block)
                total = jnp.dot(
                    rows_in[slot, span, :], weights[1, :, :HW], preferred_element_type=jnp.float32
                ).astype(BF)
                for h in range(HEADS):
                    queries[h, span, :HS] = total[:, h * HS : (h + 1) * HS]
                return 0

            lax.fori_loop(0, ROWS // block, make_queries, 0)
            for side in range(4):

                @pl.when(info_ref[SOURCE + 4 * slot + side] != NONE)
                def _(side=side):
                    target = rows_in.at[slot, pl.ds(ROWS + side * STRIP, STRIP), :]
                    pltpu.make_async_copy(rims[0], target, row_sems.at[slot, side]).wait()

            wait_weights(0)

            def make_keys(i, _):
                span = pl.ds(pl.multiple_of(i * block, block), block)
                total = jnp.dot(
                    rows_in[slot, span, :], weights[0], preferred_element_type=jnp.float32
                ).astype(BF)
                for h in range(HEADS):
                    keys[h, span, :HS] = total[:, h * HS : (h + 1) * HS]
                    values[h, span, :HS] = total[:, HW + h * HS : HW + (h + 1) * HS]
                return 0

            lax.fori_loop(0, KEYS // block, make_keys, 0)
            for h in range(HEADS):
                scores = lax.dot_general(
                    queries[h], keys[h], dims, preferred_element_type=jnp.float32
                )
                highest = jnp.max(scores, -1, keepdims=True)
                share = jnp.exp2((scores - highest) * factor).astype(BF)
                total = jnp.dot(share, values[h], preferred_element_type=jnp.float32)
                total = total[:, :HS] * (1.0 / total[:, HS : HS + 1])
                mixed[:, LEAD + h * HS : LEAD + (h + 1) * HS] = total.astype(BF)

            def project(i, _):
                span = pl.ds(pl.multiple_of(i * block, block), block)
                total = lax.dot_general(
                    mixed[span, :],
                    weights[1, :, HW - LEAD :],
                    dims,
                    preferred_element_type=jnp.float32,
                )
                out_ref[slot, span, :] = total.astype(BF)
                return 0

            lax.fori_loop(0, ROWS // block, project, 0)

        @pl.when(jnp.logical_not(live))
        def _():
            out_ref[slot] = jnp.zeros(out_ref.shape[1:], BF)

        return 0

    lax.fori_loop(0, HOLD, work, 0)


def branch(info, mask, normed, strips, late, rims, close, mine, other, far, far_other):
    width = normed.shape[2]
    pieces = len(mine)
    anywhere = pl.BlockSpec(memory_space=pl.ANY)
    vmem = pl.BlockSpec(memory_space=pltpu.VMEM)
    smem = pl.BlockSpec(memory_space=pltpu.SMEM)
    return pl.pallas_call(
        functools.partial(branch_kernel, pieces),
        out_shape=jax.ShapeDtypeStruct(normed.shape, BF),
        in_specs=[smem, vmem] + [anywhere] * (3 + ROUNDS + NEAR + 4 * pieces - 2),
        out_specs=vmem,
        scratch_shapes=[
            pltpu.VMEM((HOLD, KEYS, width), BF),
            pltpu.VMEM((2, width, 2 * HW), BF),
            pltpu.VMEM((HEADS, KEYS, LANES), BF),
            pltpu.VMEM((HEADS, KEYS, LANES), BF),
            pltpu.VMEM((HEADS, ROWS, LANES), BF),
            pltpu.VMEM((ROWS, LEAD + HW), BF),
            pltpu.SemaphoreType.DMA((2, 2 * pieces)),
            pltpu.SemaphoreType.DMA((HOLD, 5)),
        ],
        compiler_params=pltpu.CompilerParams(vmem_limit_bytes=60 * 1024 * 1024),
        name="branch",
    )(info, mask, normed, strips, late, *rims, *close, *mine, *other, *far, *far_other)


def unused(shape):
    def kernel(out_ref):
        pass

    return pl.pallas_call(
        kernel,
        out_shape=jax.ShapeDtypeStruct(shape, BF),
        out_specs=pl.BlockSpec(memory_space=pl.ANY),
        name="unused",
    )()


def meet(choice, block, count, otherwise):
    def way(r):
        pairs = [(t, t ^ r) for t in range(count) if t ^ r < count]
        return lambda items: lax.ppermute(items[0], "tiles", pairs)

    ways = [lambda items: items[1]] + [way(r) for r in range(1, count)]
    return lax.switch(choice, ways, (block, otherwise))


def shards(tokens, padding, plan, neighbours, norm_gain, attention_weight, output_weight):
    count = lax.axis_size("tiles")
    chips = count // 2
    position = lax.axis_index("tiles")
    core = position % 2
    width = tokens.shape[2]
    rows = 2 * attention_weight.shape[0]
    info, mask = route(plan, neighbours, position, padding, rows)
    key_part = attention_weight[:, HW:]
    other_part = jnp.concatenate([attention_weight[:, :HW], output_weight.T], 1)
    nothing = jnp.zeros((STRIP, width), BF)

    def exchange(r, strips):
        block = lax.dynamic_index_in_dim(strips, info[SEND + r], 0, keepdims=False)
        return meet(info[MEET + r], block, count, nothing)

    def meet_round(r, sends):
        return meet(info[MEET + r], sends[NEAR + r], count, nothing)

    def give(sends):
        result = []
        for r in range(1, NEAR + 1):
            pairs = [(t, t ^ r) for t in range(count) if t ^ r < count]
            result.append(lax.ppermute(sends[r - 1], "tiles", pairs))
        return result

    if chips > 8:
        far, far_other = [], []
        normed, strips, *sends = prepare(tokens, norm_gain[None, :], info)
        close = give(sends)
        rims = lax.map(lambda r: exchange(r, strips), jnp.arange(ROUNDS, dtype=jnp.int32))
        rims = [rims[r] for r in range(ROUNDS)]
        mine = [lax.all_gather(key_part, "tiles", axis=0, tiled=True)]
        other = [lax.all_gather(other_part, "tiles", axis=0, tiled=True)]
    else:
        order, forward = ring_pairs(count)
        backward = [(b, a) for a, b in forward]
        swap = [(t, t ^ 1) for t in range(count)]
        kept = jnp.where(core == 0, key_part, other_part)
        given = jnp.where(core == 0, other_part, key_part)
        peer = lax.ppermute(given, "tiles", swap)
        block = jnp.concatenate(
            [jnp.where(core == 0, kept, peer), jnp.where(core == 0, peer, kept)], 0
        )
        payload = jnp.where(lax.axis_index("groups") == 0, block[:, :PART], block[:, REST:])
        across = [(0, 1), (1, 0)]
        rims, close = [], []
        near, far, swapped = [block], [], {}
        ahead = behind = payload
        crossing, waiting = [], [("near", 0)]
        last = chips // 2
        step = 0
        while step < last or crossing or waiting:
            step += 1
            arrived, met = [], []
            if step <= last:
                ahead = lax.ppermute(ahead, "tiles", forward)
                arrived = [ahead]
                if 2 * step < chips:
                    behind = lax.ppermute(behind, "tiles", backward)
                    arrived += [behind]
            crossed = [lax.ppermute(near[i], "groups", across) for i in crossing]
            free = max(4 - len(arrived) - len(crossed), 0)
            turn, waiting = waiting[:free], waiting[free:]
            pool = {"near": near, "far": far}
            peers = [lax.ppermute(pool[kind][i], "tiles", swap) for kind, i in turn]
            if step == 1:
                normed, strips, *sends = prepare(tokens, norm_gain[None, :], info)
            elif step - 2 < ROUNDS:
                met = [meet_round(step - 2, sends)]
            arrived, sends, crossed, peers, met = lax.optimization_barrier(
                (arrived, sends, crossed, peers, met)
            )
            swapped.update(zip(turn, peers))
            waiting += [("far", len(far) + i) for i in range(len(crossed))]
            waiting += [("near", len(near) + i) for i in range(len(arrived))]
            crossing = range(len(near), len(near) + len(arrived))
            near += arrived
            far += crossed
            rims += met
            if step <= last:
                ahead, behind = arrived[0], arrived[-1]
        rims += [meet_round(r, sends) for r in range(len(rims), ROUNDS)]
        mine, other = near, [swapped["near", i] for i in range(len(near))]
        far_other = [swapped["far", i] for i in range(len(far))]

    late = lax.cond(
        info[LATE] == 1,
        lambda: lax.map(lambda r: exchange(r, strips), jnp.arange(ROUNDS, MOST, dtype=jnp.int32)),
        lambda: unused((MOST - ROUNDS, STRIP, width)),
    )
    return branch(info, mask, normed, strips, late, rims, close, mine, other, far, far_other)


def solution(mesh):
    return jax.shard_map(
        shards,
        mesh=mesh,
        in_specs=(
            P(("groups", "tiles"), None, None),
            P("groups", None),
            P("groups"),
            P("groups", None),
            P(),
            P("tiles", None),
            P(None, "tiles"),
        ),
        out_specs=P(("groups", "tiles"), None, None),
        check_vma=False,
    )
```

```python
import functools
import math

import jax
import jax.numpy as jnp
from jax import lax
from jax.experimental import pallas as pl
from jax.experimental.pallas import tpu as pltpu
from jax.sharding import PartitionSpec as P

HEADS = 8
HS = 104
HW = HEADS * HS
SIDE = 32
HALF = 16
RIM = 4
ROWS = 512
STRIP = 128
KEYS = ROWS + 4 * STRIP
HOLD = 2
LANES = 128
LEAD = 64
BF = jnp.bfloat16
PART = (2 * HW // LANES + 1) // 2 * LANES
REST = 2 * HW - PART

ROUNDS, MOST = 8, 15
MEET, SEND, SOURCE, LIVE, LATE, CORE, PLACE, GROUP, WHOLE = 0, 16, 32, 40, 42, 43, 44, 52, 53
LOCAL, NONE = 16, 32


def routing(count, rows, plan_ref, beside_ref, padding_ref, out_ref, mask_ref, live, used, color, tally, edges):
    me = lax.axis_index("tiles")
    slots = HOLD * count

    def clear(s, _):
        live[s] = 0
        return 0

    lax.fori_loop(0, slots, clear, 0, unroll=8)

    def mark(j, _):
        live[plan_ref[j]] = 1
        return 0

    lax.fori_loop(0, count, mark, 0, unroll=8)

    def empty(t, _):
        used[t] = 0
        return 0

    lax.fori_loop(0, count, empty, 0, unroll=8)

    for weight in range(3):
        tally[weight] = 0

    def collect(e, _):
        s = lax.shift_right_logical(e, 1)
        side = 1 + 2 * jnp.bitwise_and(e, 1)
        n = beside_ref[s, side]
        safe = jnp.maximum(n, 0)
        a, b = lax.shift_right_logical(s, 1), lax.shift_right_logical(safe, 1)

        @pl.when((n >= 0) & (a != b))
        def _():
            heavy = live[2 * a] * live[2 * a + 1] + live[2 * b] * live[2 * b + 1]
            place = tally[heavy]
            edges[2 * slots * heavy + place] = 4 * s + side
            tally[heavy] = place + 1

        return 0

    lax.fori_loop(0, 2 * slots, collect, 0, unroll=4)
    for weight in (2, 1, 0):

        def edge(e, _, weight=weight):
            key = edges[2 * slots * weight + e]
            s = lax.shift_right_logical(key, 2)
            side = jnp.bitwise_and(key, 3)
            n = beside_ref[s, side]
            a, b = lax.shift_right_logical(s, 1), lax.shift_right_logical(n, 1)
            taken = jnp.bitwise_or(used[a], used[b])
            first = lax.while_loop(
                lambda c: jnp.bitwise_and(lax.shift_right_logical(taken, c), 1) == 1,
                lambda c: c + 1,
                jnp.int32(0),
            )
            bit = lax.shift_left(jnp.int32(1), first)
            used[a] = jnp.bitwise_or(used[a], bit)
            used[b] = jnp.bitwise_or(used[b], bit)
            color[key] = first
            color[4 * n + jnp.bitwise_xor(side, 1)] = first
            return 0

        lax.fori_loop(0, tally[weight], edge, 0)

    for r in range(MOST + 1):
        out_ref[MEET + r] = 0
        out_ref[SEND + r] = 0
    out_ref[LATE] = 0
    out_ref[WHOLE] = 0
    for i in range(HOLD):
        slot = HOLD * me + i
        out_ref[LIVE + i] = live[slot]
        mask_ref[i : i + 1, :ROWS] = padding_ref[pl.ds(slot, 1), :].astype(jnp.float32)
        for side in range(4):
            n = beside_ref[slot, side]
            has = (n >= 0) & (live[slot] == 1)
            safe = jnp.maximum(n, 0)
            other = lax.shift_right_logical(safe, 1)
            away = has & (other != me)
            out_ref[SOURCE + 4 * i + side] = jnp.where(has, LOCAL + 4 * jnp.bitwise_and(safe, 1) + side, NONE)

            @pl.when(away)
            def _(i=i, side=side, slot=slot, other=other):
                c = color[4 * slot + side]
                out_ref[SOURCE + 4 * i + side] = c
                out_ref[MEET + c] = jnp.bitwise_xor(other, me)
                out_ref[SEND + c] = 4 * i + (side ^ 1)

                @pl.when(c >= ROUNDS)
                def _():
                    out_ref[LATE] = 1
                    out_ref[WHOLE] = 1

            @pl.when(has & (other == me))
            def _():
                out_ref[WHOLE] = 1

            row_live = padding_ref[pl.ds(safe, 1), :].astype(jnp.float32)
            if side < 2:
                token = lax.broadcasted_iota(jnp.int32, (ROWS, STRIP), 0)
                place = lax.broadcasted_iota(jnp.int32, (ROWS, STRIP), 1)
                band = 2 * RIM
                wanted = lax.shift_right_logical(place, 3) * SIDE + jnp.bitwise_and(place, band - 1)
                wanted = wanted + (SIDE - band if side == 0 else 0)
                chosen = jnp.where(token == wanted, 1.0, 0.0).astype(BF)
                strip = jnp.dot(row_live.astype(BF), chosen, preferred_element_type=jnp.float32)
            else:
                strip = row_live[:, ROWS - STRIP :] if side == 2 else row_live[:, :STRIP]
            begin = ROWS + side * STRIP
            mask_ref[i : i + 1, begin : begin + STRIP] = jnp.where(has, strip, 0.0)

    core = jnp.bitwise_and(me, 1)
    chip = lax.shift_right_logical(me, 1)
    chips = count // 2
    order, _ = ring_pairs(count)
    plan_of_ring = ring_steps(chips)
    out_ref[CORE] = core if len(plan_of_ring) > 1 else jnp.int32(0)
    out_ref[GROUP] = lax.axis_index("groups")
    for index, step in enumerate(plan_of_ring):
        start = jnp.int32(0)
        if len(plan_of_ring) > 1:
            for rank, c in enumerate(order):
                start = jnp.where(chip == c, order[(rank + step) % chips] * rows, start)
        out_ref[PLACE + index] = start


def ring_pairs(count):
    chips = count // 2
    order = list(range(0, chips, 2)) + list(range(chips - 1 - chips % 2, 0, -2))
    forward = []
    for index, chip in enumerate(order):
        after = order[(index + 1) % chips]
        forward += [(2 * chip + c, 2 * after + c) for c in range(2)]
    return order, forward


def ring_steps(chips):
    if chips > 8:
        return [0]
    pieces = [0]
    for step in range(1, chips // 2 + 1):
        pieces += [-step, step] if 2 * step < chips else [-step]
    return pieces


def route(plan, neighbours, padding, rows):
    count = plan.shape[0]
    smem = pl.BlockSpec(memory_space=pltpu.SMEM)
    vmem = pl.BlockSpec(memory_space=pltpu.VMEM)
    return pl.pallas_call(
        functools.partial(routing, count, rows),
        out_shape=(
            jax.ShapeDtypeStruct((64,), jnp.int32),
            jax.ShapeDtypeStruct((HOLD, KEYS), jnp.float32),
        ),
        in_specs=[smem] * 2 + [vmem],
        out_specs=(smem, vmem),
        scratch_shapes=[
            pltpu.SMEM((HOLD * count,), jnp.int32),
            pltpu.SMEM((count,), jnp.int32),
            pltpu.SMEM((4 * HOLD * count,), jnp.int32),
            pltpu.SMEM((3,), jnp.int32),
            pltpu.SMEM((6 * HOLD * count,), jnp.int32),
        ],
        name="routing",
    )(plan, neighbours, padding)


def prepare_kernel(tokens_ref, gain_ref, info_ref, normed_ref, strips_ref, *rest):
    sends, (work, normed, strips, in_sems, out_sems, send_sems) = rest[:ROUNDS], rest[ROUNDS:]
    gain = gain_ref[...]
    band = 2 * RIM
    lives = [info_ref[LIVE + slot] == 1 for slot in range(HOLD)]

    def fetch(slot):
        return pltpu.make_async_copy(tokens_ref.at[slot], work.at[slot], in_sems.at[slot])

    def keep(slot):
        return pltpu.make_async_copy(normed.at[slot], normed_ref.at[slot], out_sems.at[slot])

    def keep_strips():
        return pltpu.make_async_copy(strips, strips_ref, out_sems.at[HOLD])

    def send(r):
        return pltpu.make_async_copy(strips.at[info_ref[SEND + r]], sends[r], send_sems.at[r])

    def normal(values):
        offset = values - jnp.mean(values, -1, keepdims=True)
        spread = jnp.mean(offset * offset, -1, keepdims=True)
        return offset * lax.rsqrt(spread + 1e-06) * gain

    for slot in range(HOLD):

        @pl.when(lives[slot])
        def _(slot=slot):
            fetch(slot).start()

    for slot in range(HOLD):

        @pl.when(lives[slot])
        def _(slot=slot):
            fetch(slot).wait()

            def pair(i, _):
                lines = []
                for half in range(2):
                    span = pl.ds(pl.multiple_of((2 * i + half) * SIDE, SIDE), SIDE)
                    line = normal(work[slot, span, :].astype(jnp.float32))
                    normed[slot, span, :] = line.astype(BF)
                    lines.append(line)
                span = pl.ds(pl.multiple_of(i * 2 * band, 2 * band), 2 * band)
                last = jnp.concatenate([line[SIDE - band :] for line in lines], 0)
                first = jnp.concatenate([line[:band] for line in lines], 0)
                strips[4 * slot, span, :] = last.astype(BF)
                strips[4 * slot + 1, span, :] = first.astype(BF)
                return 0

            lax.fori_loop(0, HALF // 2, pair, 0, unroll=4)
            strips[4 * slot + 2] = normed[slot, ROWS - STRIP :, :]
            strips[4 * slot + 3] = normed[slot, :STRIP, :]
            keep(slot).start()

    whole = info_ref[WHOLE] == 1

    @pl.when(whole)
    def _():
        keep_strips().start()

    for r in range(ROUNDS):

        @pl.when(info_ref[MEET + r] != 0)
        def _(r=r):
            send(r).start()

    for r in range(ROUNDS):

        @pl.when(info_ref[MEET + r] != 0)
        def _(r=r):
            send(r).wait()

    @pl.when(whole)
    def _():
        keep_strips().wait()

    for slot in range(HOLD):

        @pl.when(lives[slot])
        def _(slot=slot):
            keep(slot).wait()


def prepare(tokens, gain, info):
    width = tokens.shape[-1]
    anywhere = pl.BlockSpec(memory_space=pl.ANY)
    vmem = pl.BlockSpec(memory_space=pltpu.VMEM)
    smem = pl.BlockSpec(memory_space=pltpu.SMEM)
    return pl.pallas_call(
        prepare_kernel,
        out_shape=(
            jax.ShapeDtypeStruct(tokens.shape, BF),
            jax.ShapeDtypeStruct((4 * HOLD, STRIP, width), BF),
        )
        + (jax.ShapeDtypeStruct((STRIP, width), BF),) * ROUNDS,
        in_specs=[anywhere, vmem, smem],
        out_specs=(anywhere,) * (2 + ROUNDS),
        scratch_shapes=[
            pltpu.VMEM(tokens.shape, BF),
            pltpu.VMEM(tokens.shape, BF),
            pltpu.VMEM((4 * HOLD, STRIP, width), BF),
            pltpu.SemaphoreType.DMA((HOLD,)),
            pltpu.SemaphoreType.DMA((HOLD + 1,)),
            pltpu.SemaphoreType.DMA((ROUNDS,)),
        ],
        compiler_params=pltpu.CompilerParams(vmem_limit_bytes=60 * 1024 * 1024),
        name="prepare",
    )(tokens, gain, info)


def branch_kernel(pieces, *refs):
    info_ref, mask_ref, normed_ref, strips_ref, late_ref = refs[:5]
    rims = refs[5 : 5 + ROUNDS]
    refs = refs[5 + ROUNDS :]
    mine, other = refs[:pieces], refs[pieces : 2 * pieces]
    refs = refs[2 * pieces :]
    far, far_other = refs[: pieces - 1], refs[pieces - 1 : 2 * pieces - 2]
    out_ref, rows_in, weights, keys, values, queries, mixed, sems, row_sems = refs[2 * pieces - 2 :]
    core, group = info_ref[CORE], info_ref[GROUP]

    def weight_copies(half, near, beyond):
        for i in range(pieces):
            target = weights.at[half, pl.ds(pl.multiple_of(info_ref[PLACE + i], 16), near[i].shape[0])]
            if i == 0:
                yield pltpu.make_async_copy(near[0], target, sems.at[half, 0])
                continue
            start = pl.multiple_of(group * REST, LANES)
            part = target.at[:, pl.ds(start, PART)]
            yield pltpu.make_async_copy(near[i], part, sems.at[half, 2 * i])
            first = pl.multiple_of((1 - group) * (PART - REST), LANES)
            source = beyond[i - 1].at[:, pl.ds(first, REST)]
            rest = target.at[:, pl.ds(pl.multiple_of((1 - group) * PART, LANES), REST)]
            yield pltpu.make_async_copy(source, rest, sems.at[half, 2 * i - 1])

    def start_weights(half):
        @pl.when(core == half)
        def _():
            for copy in weight_copies(half, mine, far):
                copy.start()

        @pl.when(core != half)
        def _():
            for copy in weight_copies(half, other, far_other):
                copy.start()

    for slot in range(HOLD):

        @pl.when(info_ref[LIVE + slot] == 1)
        def _(slot=slot):
            target = rows_in.at[slot, pl.ds(0, ROWS), :]
            pltpu.make_async_copy(normed_ref.at[slot], target, row_sems.at[slot, 4]).start()

    busy = info_ref[LIVE] + info_ref[LIVE + 1] > 0

    @pl.when(busy)
    def _():
        start_weights(1)
        start_weights(0)

    for slot in range(HOLD):

        @pl.when(info_ref[LIVE + slot] == 1)
        def _(slot=slot):
            for side in range(4):
                source = info_ref[SOURCE + 4 * slot + side]
                span = pl.ds(ROWS + side * STRIP, STRIP)
                target = rows_in.at[slot, span, :]
                sem = row_sems.at[slot, side]
                for r in range(ROUNDS):

                    @pl.when(source == r)
                    def _(r=r, target=target, sem=sem):
                        pltpu.make_async_copy(rims[r], target, sem).start()

                @pl.when((source >= ROUNDS) & (source < MOST))
                def _(source=source, target=target, sem=sem):
                    pltpu.make_async_copy(late_ref.at[source - ROUNDS], target, sem).start()

                @pl.when((source >= LOCAL) & (source < NONE))
                def _(source=source, target=target, sem=sem):
                    pltpu.make_async_copy(strips_ref.at[source - LOCAL], target, sem).start()

                @pl.when(source == NONE)
                def _(slot=slot, span=span):
                    rows_in[slot, span, :] = jnp.zeros((STRIP, rows_in.shape[2]), BF)

    block = 512
    factor = math.log2(math.e) / math.sqrt(HS)
    dims = (((1,), (1,)), ((), ()))
    mixed[:, :LEAD] = jnp.zeros((ROWS, LEAD), BF)
    lane = lax.broadcasted_iota(jnp.int32, (KEYS, LANES), 1)
    one = jnp.where(lane == HS, 1.0, 0.0).astype(BF)
    for h in range(HEADS):
        queries[h] = one[:ROWS]
        values[h] = one

    def work(slot, _):
        live = info_ref[LIVE + slot] == 1

        @pl.when(live)
        def _():
            away = jnp.where(mask_ref[pl.ds(slot, 1), :] > 0.5, 0.0, -1e30)
            away = jnp.broadcast_to(away, (LANES, KEYS)).T
            away = jnp.where(lane == HS, away, 0.0).astype(BF)
            for h in range(HEADS):
                keys[h] = away
            initial = (slot == 0) | (info_ref[LIVE] == 0)

            def wait_weights(half):
                @pl.when(initial)
                def _():
                    for copy in weight_copies(half, mine, far):
                        copy.wait()

            target = rows_in.at[slot, pl.ds(0, ROWS), :]
            pltpu.make_async_copy(normed_ref.at[slot], target, row_sems.at[slot, 4]).wait()
            wait_weights(1)

            def make_queries(i, _):
                span = pl.ds(pl.multiple_of(i * block, block), block)
                total = jnp.dot(
                    rows_in[slot, span, :], weights[1, :, :HW], preferred_element_type=jnp.float32
                ).astype(BF)
                for h in range(HEADS):
                    queries[h, span, :HS] = total[:, h * HS : (h + 1) * HS]
                return 0

            lax.fori_loop(0, ROWS // block, make_queries, 0)
            for side in range(4):

                @pl.when(info_ref[SOURCE + 4 * slot + side] != NONE)
                def _(side=side):
                    target = rows_in.at[slot, pl.ds(ROWS + side * STRIP, STRIP), :]
                    pltpu.make_async_copy(rims[0], target, row_sems.at[slot, side]).wait()

            wait_weights(0)

            def make_keys(i, _):
                span = pl.ds(pl.multiple_of(i * block, block), block)
                total = jnp.dot(
                    rows_in[slot, span, :], weights[0], preferred_element_type=jnp.float32
                ).astype(BF)
                for h in range(HEADS):
                    keys[h, span, :HS] = total[:, h * HS : (h + 1) * HS]
                    values[h, span, :HS] = total[:, HW + h * HS : HW + (h + 1) * HS]
                return 0

            lax.fori_loop(0, KEYS // block, make_keys, 0)
            for h in range(HEADS):
                scores = lax.dot_general(
                    queries[h], keys[h], dims, preferred_element_type=jnp.float32
                )
                highest = jnp.max(scores, -1, keepdims=True)
                share = jnp.exp2((scores - highest) * factor).astype(BF)
                total = jnp.dot(share, values[h], preferred_element_type=jnp.float32)
                total = total[:, :HS] * (1.0 / total[:, HS : HS + 1])
                mixed[:, LEAD + h * HS : LEAD + (h + 1) * HS] = total.astype(BF)

            def project(i, _):
                span = pl.ds(pl.multiple_of(i * block, block), block)
                total = lax.dot_general(
                    mixed[span, :],
                    weights[1, :, HW - LEAD :],
                    dims,
                    preferred_element_type=jnp.float32,
                )
                out_ref[slot, span, :] = total.astype(BF)
                return 0

            lax.fori_loop(0, ROWS // block, project, 0)

        @pl.when(jnp.logical_not(live))
        def _():
            out_ref[slot] = jnp.zeros(out_ref.shape[1:], BF)

        return 0

    lax.fori_loop(0, HOLD, work, 0)


def branch(info, mask, normed, strips, late, rims, mine, other, far, far_other):
    width = normed.shape[2]
    pieces = len(mine)
    anywhere = pl.BlockSpec(memory_space=pl.ANY)
    vmem = pl.BlockSpec(memory_space=pltpu.VMEM)
    smem = pl.BlockSpec(memory_space=pltpu.SMEM)
    return pl.pallas_call(
        functools.partial(branch_kernel, pieces),
        out_shape=jax.ShapeDtypeStruct(normed.shape, BF),
        in_specs=[smem, vmem] + [anywhere] * (3 + ROUNDS + 4 * pieces - 2),
        out_specs=vmem,
        scratch_shapes=[
            pltpu.VMEM((HOLD, KEYS, width), BF),
            pltpu.VMEM((2, width, 2 * HW), BF),
            pltpu.VMEM((HEADS, KEYS, LANES), BF),
            pltpu.VMEM((HEADS, KEYS, LANES), BF),
            pltpu.VMEM((HEADS, ROWS, LANES), BF),
            pltpu.VMEM((ROWS, LEAD + HW), BF),
            pltpu.SemaphoreType.DMA((2, 2 * pieces)),
            pltpu.SemaphoreType.DMA((HOLD, 5)),
        ],
        compiler_params=pltpu.CompilerParams(vmem_limit_bytes=60 * 1024 * 1024),
        name="branch",
    )(info, mask, normed, strips, late, *rims, *mine, *other, *far, *far_other)


def unused(shape):
    def kernel(out_ref):
        pass

    return pl.pallas_call(
        kernel,
        out_shape=jax.ShapeDtypeStruct(shape, BF),
        out_specs=pl.BlockSpec(memory_space=pl.ANY),
        name="unused",
    )()


def meet(choice, block, count):
    def way(r):
        pairs = [(t, t ^ r) for t in range(count) if t ^ r < count]
        return lambda items: lax.ppermute(items[0], "tiles", pairs)

    ways = [lambda items: unused(items[0].shape)] + [way(r) for r in range(1, count)]
    return lax.switch(choice, ways, (block,))


def shards(tokens, padding, plan, neighbours, norm_gain, attention_weight, output_weight):
    count = lax.axis_size("tiles")
    chips = count // 2
    position = lax.axis_index("tiles")
    core = position % 2
    width = tokens.shape[2]
    rows = 2 * attention_weight.shape[0]
    info, mask = route(plan, neighbours, padding, rows)
    key_part = attention_weight[:, HW:]
    other_part = jnp.concatenate([attention_weight[:, :HW], output_weight.T], 1)

    def exchange(r, strips):
        block = lax.dynamic_index_in_dim(strips, info[SEND + r], 0, keepdims=False)
        return meet(info[MEET + r], block, count)

    def meet_round(r, sends):
        return meet(info[MEET + r], sends[r], count)

    if chips > 8:
        far, far_other = [], []
        normed, strips, *sends = prepare(tokens, norm_gain[None, :], info)
        rims = lax.map(lambda r: exchange(r, strips), jnp.arange(ROUNDS, dtype=jnp.int32))
        rims = [rims[r] for r in range(ROUNDS)]
        mine = [lax.all_gather(key_part, "tiles", axis=0, tiled=True)]
        other = [lax.all_gather(other_part, "tiles", axis=0, tiled=True)]
    else:
        order, forward = ring_pairs(count)
        backward = [(b, a) for a, b in forward]
        swap = [(t, t ^ 1) for t in range(count)]
        kept = jnp.where(core == 0, key_part, other_part)
        given = jnp.where(core == 0, other_part, key_part)
        peer = lax.ppermute(given, "tiles", swap)
        block = jnp.concatenate(
            [jnp.where(core == 0, kept, peer), jnp.where(core == 0, peer, kept)], 0
        )
        payload = jnp.where(lax.axis_index("groups") == 0, block[:, :PART], block[:, REST:])
        across = [(0, 1), (1, 0)]
        rims = []
        near, far, swapped = [block], [], {}
        ahead = behind = payload
        crossing, waiting = [], [("near", 0)]
        last = chips // 2
        step = 0
        while step < last or crossing or waiting:
            step += 1
            arrived, met = [], []
            if step <= last:
                ahead = lax.ppermute(ahead, "tiles", forward)
                arrived = [ahead]
                if 2 * step < chips:
                    behind = lax.ppermute(behind, "tiles", backward)
                    arrived += [behind]
            crossed = [lax.ppermute(near[i], "groups", across) for i in crossing]
            free = max(4 - len(arrived) - len(crossed), 0)
            turn, waiting = waiting[:free], waiting[free:]
            pool = {"near": near, "far": far}
            peers = [lax.ppermute(pool[kind][i], "tiles", swap) for kind, i in turn]
            if step == 1:
                normed, strips, *sends = prepare(tokens, norm_gain[None, :], info)
            elif step - 2 < ROUNDS:
                met = [meet_round(step - 2, sends)]
            arrived, sends, crossed, peers, met = lax.optimization_barrier(
                (arrived, sends, crossed, peers, met)
            )
            swapped.update(zip(turn, peers))
            waiting += [("far", len(far) + i) for i in range(len(crossed))]
            waiting += [("near", len(near) + i) for i in range(len(arrived))]
            crossing = range(len(near), len(near) + len(arrived))
            near += arrived
            far += crossed
            rims += met
            if step <= last:
                ahead, behind = arrived[0], arrived[-1]
        rims += [meet_round(r, sends) for r in range(len(rims), ROUNDS)]
        mine, other = near, [swapped["near", i] for i in range(len(near))]
        far_other = [swapped["far", i] for i in range(len(far))]

    late = lax.cond(
        info[LATE] == 1,
        lambda: lax.map(lambda r: exchange(r, strips), jnp.arange(ROUNDS, MOST, dtype=jnp.int32)),
        lambda: unused((MOST - ROUNDS, STRIP, width)),
    )
    return branch(info, mask, normed, strips, late, rims, mine, other, far, far_other)


def solution(mesh):
    return jax.shard_map(
        shards,
        mesh=mesh,
        in_specs=(
            P(("groups", "tiles"), None, None),
            P("groups", None),
            P("groups"),
            P("groups", None),
            P(),
            P("tiles", None),
            P(None, "tiles"),
        ),
        out_specs=P(("groups", "tiles"), None, None),
        check_vma=False,
    )
```

```python
import functools
import math

import jax
import jax.numpy as jnp
from jax import lax
from jax.experimental import pallas as pl
from jax.experimental.pallas import tpu as pltpu
from jax.sharding import PartitionSpec as P

HEADS = 8
HS = 104
HW = HEADS * HS
SIDE = 32
HALF = 16
RIM = 4
ROWS = 512
STRIP = 128
KEYS = ROWS + 4 * STRIP
HOLD = 2
LANES = 128
LEAD = 64
BF = jnp.bfloat16
PART = (2 * HW // LANES + 1) // 2 * LANES
REST = 2 * HW - PART

ROUNDS, MOST = 8, 15
MEET, SEND, SOURCE, LIVE, LATE, CORE, PLACE, GROUP, WHOLE = 0, 16, 32, 40, 42, 43, 44, 52, 53
LOCAL, NONE = 16, 32


def routing(count, rows, plan_ref, beside_ref, padding_ref, out_ref, mask_ref, live, used, color, tally, edges):
    me = lax.axis_index("tiles")
    slots = HOLD * count

    def clear(s, _):
        live[s] = 0
        return 0

    lax.fori_loop(0, slots, clear, 0, unroll=8)

    def mark(j, _):
        live[plan_ref[j]] = 1
        return 0

    lax.fori_loop(0, count, mark, 0, unroll=8)

    def empty(t, _):
        used[t] = 0
        return 0

    lax.fori_loop(0, count, empty, 0, unroll=8)

    for weight in range(3):
        tally[weight] = 0

    def collect(e, _):
        s = lax.shift_right_logical(e, 1)
        side = 1 + 2 * jnp.bitwise_and(e, 1)
        n = beside_ref[s, side]
        safe = jnp.maximum(n, 0)
        a, b = lax.shift_right_logical(s, 1), lax.shift_right_logical(safe, 1)

        @pl.when((n >= 0) & (a != b))
        def _():
            heavy = live[2 * a] * live[2 * a + 1] + live[2 * b] * live[2 * b + 1]
            place = tally[heavy]
            edges[2 * slots * heavy + place] = 4 * s + side
            tally[heavy] = place + 1

        return 0

    lax.fori_loop(0, 2 * slots, collect, 0, unroll=4)
    for weight in (2, 1, 0):

        def edge(e, _, weight=weight):
            key = edges[2 * slots * weight + e]
            s = lax.shift_right_logical(key, 2)
            side = jnp.bitwise_and(key, 3)
            n = beside_ref[s, side]
            a, b = lax.shift_right_logical(s, 1), lax.shift_right_logical(n, 1)
            taken = jnp.bitwise_or(used[a], used[b])
            first = lax.while_loop(
                lambda c: jnp.bitwise_and(lax.shift_right_logical(taken, c), 1) == 1,
                lambda c: c + 1,
                jnp.int32(0),
            )
            bit = lax.shift_left(jnp.int32(1), first)
            used[a] = jnp.bitwise_or(used[a], bit)
            used[b] = jnp.bitwise_or(used[b], bit)
            color[key] = first
            color[4 * n + jnp.bitwise_xor(side, 1)] = first
            return 0

        lax.fori_loop(0, tally[weight], edge, 0)

    for r in range(MOST + 1):
        out_ref[MEET + r] = 0
        out_ref[SEND + r] = 0
    out_ref[LATE] = 0
    out_ref[WHOLE] = 0
    for i in range(HOLD):
        slot = HOLD * me + i
        out_ref[LIVE + i] = live[slot]
        mask_ref[i : i + 1, :ROWS] = padding_ref[pl.ds(slot, 1), :].astype(jnp.float32)
        for side in range(4):
            n = beside_ref[slot, side]
            has = (n >= 0) & (live[slot] == 1)
            safe = jnp.maximum(n, 0)
            other = lax.shift_right_logical(safe, 1)
            away = has & (other != me)
            out_ref[SOURCE + 4 * i + side] = jnp.where(has, LOCAL + 4 * jnp.bitwise_and(safe, 1) + side, NONE)

            @pl.when(away)
            def _(i=i, side=side, slot=slot, other=other):
                c = color[4 * slot + side]
                out_ref[SOURCE + 4 * i + side] = c
                out_ref[MEET + c] = jnp.bitwise_xor(other, me)
                out_ref[SEND + c] = 4 * i + (side ^ 1)

                @pl.when(c >= ROUNDS)
                def _():
                    out_ref[LATE] = 1
                    out_ref[WHOLE] = 1

            @pl.when(has & (other == me))
            def _():
                out_ref[WHOLE] = 1

            row_live = padding_ref[pl.ds(safe, 1), :].astype(jnp.float32)
            if side < 2:
                token = lax.broadcasted_iota(jnp.int32, (ROWS, STRIP), 0)
                place = lax.broadcasted_iota(jnp.int32, (ROWS, STRIP), 1)
                band = 2 * RIM
                wanted = lax.shift_right_logical(place, 3) * SIDE + jnp.bitwise_and(place, band - 1)
                wanted = wanted + (SIDE - band if side == 0 else 0)
                chosen = jnp.where(token == wanted, 1.0, 0.0).astype(BF)
                strip = jnp.dot(row_live.astype(BF), chosen, preferred_element_type=jnp.float32)
            else:
                strip = row_live[:, ROWS - STRIP :] if side == 2 else row_live[:, :STRIP]
            begin = ROWS + side * STRIP
            mask_ref[i : i + 1, begin : begin + STRIP] = jnp.where(has, strip, 0.0)

    core = jnp.bitwise_and(me, 1)
    chip = lax.shift_right_logical(me, 1)
    chips = count // 2
    order, _ = ring_pairs(count)
    plan_of_ring = ring_steps(chips)
    out_ref[CORE] = core if len(plan_of_ring) > 1 else jnp.int32(0)
    out_ref[GROUP] = lax.axis_index("groups")
    for index, step in enumerate(plan_of_ring):
        start = jnp.int32(0)
        if len(plan_of_ring) > 1:
            for rank, c in enumerate(order):
                start = jnp.where(chip == c, order[(rank + step) % chips] * rows, start)
        out_ref[PLACE + index] = start


def ring_pairs(count):
    chips = count // 2
    order = list(range(0, chips, 2)) + list(range(chips - 1 - chips % 2, 0, -2))
    forward = []
    for index, chip in enumerate(order):
        after = order[(index + 1) % chips]
        forward += [(2 * chip + c, 2 * after + c) for c in range(2)]
    return order, forward


def ring_steps(chips):
    if chips > 8:
        return [0]
    pieces = [0]
    for step in range(1, chips // 2 + 1):
        pieces += [-step, step] if 2 * step < chips else [-step]
    return pieces


def route(plan, neighbours, padding, rows):
    count = plan.shape[0]
    smem = pl.BlockSpec(memory_space=pltpu.SMEM)
    vmem = pl.BlockSpec(memory_space=pltpu.VMEM)
    return pl.pallas_call(
        functools.partial(routing, count, rows),
        out_shape=(
            jax.ShapeDtypeStruct((64,), jnp.int32),
            jax.ShapeDtypeStruct((HOLD, KEYS), jnp.float32),
        ),
        in_specs=[smem] * 2 + [vmem],
        out_specs=(smem, vmem),
        scratch_shapes=[
            pltpu.SMEM((HOLD * count,), jnp.int32),
            pltpu.SMEM((count,), jnp.int32),
            pltpu.SMEM((4 * HOLD * count,), jnp.int32),
            pltpu.SMEM((3,), jnp.int32),
            pltpu.SMEM((6 * HOLD * count,), jnp.int32),
        ],
        name="routing",
    )(plan, neighbours, padding)


def prepare_kernel(tokens_ref, gain_ref, info_ref, normed_ref, strips_ref, *rest):
    sends, (work, normed, strips, in_sems, out_sems, send_sems) = rest[:ROUNDS], rest[ROUNDS:]
    gain = gain_ref[...][None, :]
    band = 2 * RIM
    lives = [info_ref[LIVE + slot] == 1 for slot in range(HOLD)]

    def fetch(slot):
        return pltpu.make_async_copy(tokens_ref.at[slot], work.at[slot], in_sems.at[slot])

    def keep(slot):
        return pltpu.make_async_copy(normed.at[slot], normed_ref.at[slot], out_sems.at[slot])

    def keep_strips():
        return pltpu.make_async_copy(strips, strips_ref, out_sems.at[HOLD])

    def send(r):
        return pltpu.make_async_copy(strips.at[info_ref[SEND + r]], sends[r], send_sems.at[r])

    def normal(values):
        offset = values - jnp.mean(values, -1, keepdims=True)
        spread = jnp.mean(offset * offset, -1, keepdims=True)
        return offset * lax.rsqrt(spread + 1e-06) * gain

    for slot in range(HOLD):

        @pl.when(lives[slot])
        def _(slot=slot):
            fetch(slot).start()

    for slot in range(HOLD):

        @pl.when(lives[slot])
        def _(slot=slot):
            fetch(slot).wait()

            def pair(i, _):
                lines = []
                for half in range(2):
                    span = pl.ds(pl.multiple_of((2 * i + half) * SIDE, SIDE), SIDE)
                    line = normal(work[slot, span, :].astype(jnp.float32))
                    normed[slot, span, :] = line.astype(BF)
                    lines.append(line)
                span = pl.ds(pl.multiple_of(i * 2 * band, 2 * band), 2 * band)
                last = jnp.concatenate([line[SIDE - band :] for line in lines], 0)
                first = jnp.concatenate([line[:band] for line in lines], 0)
                strips[4 * slot, span, :] = last.astype(BF)
                strips[4 * slot + 1, span, :] = first.astype(BF)
                return 0

            lax.fori_loop(0, HALF // 2, pair, 0, unroll=4)
            strips[4 * slot + 2] = normed[slot, ROWS - STRIP :, :]
            strips[4 * slot + 3] = normed[slot, :STRIP, :]
            keep(slot).start()

    whole = info_ref[WHOLE] == 1

    @pl.when(whole)
    def _():
        keep_strips().start()

    for r in range(ROUNDS):

        @pl.when(info_ref[MEET + r] != 0)
        def _(r=r):
            send(r).start()

    for r in range(ROUNDS):

        @pl.when(info_ref[MEET + r] != 0)
        def _(r=r):
            send(r).wait()

    @pl.when(whole)
    def _():
        keep_strips().wait()

    for slot in range(HOLD):

        @pl.when(lives[slot])
        def _(slot=slot):
            keep(slot).wait()


def prepare(tokens, gain, info):
    width = tokens.shape[-1]
    anywhere = pl.BlockSpec(memory_space=pl.ANY)
    vmem = pl.BlockSpec(memory_space=pltpu.VMEM)
    smem = pl.BlockSpec(memory_space=pltpu.SMEM)
    return pl.pallas_call(
        prepare_kernel,
        out_shape=(
            jax.ShapeDtypeStruct(tokens.shape, BF),
            jax.ShapeDtypeStruct((4 * HOLD, STRIP, width), BF),
        )
        + (jax.ShapeDtypeStruct((STRIP, width), BF),) * ROUNDS,
        in_specs=[anywhere, vmem, smem],
        out_specs=(anywhere,) * (2 + ROUNDS),
        scratch_shapes=[
            pltpu.VMEM(tokens.shape, BF),
            pltpu.VMEM(tokens.shape, BF),
            pltpu.VMEM((4 * HOLD, STRIP, width), BF),
            pltpu.SemaphoreType.DMA((HOLD,)),
            pltpu.SemaphoreType.DMA((HOLD + 1,)),
            pltpu.SemaphoreType.DMA((ROUNDS,)),
        ],
        compiler_params=pltpu.CompilerParams(vmem_limit_bytes=60 * 1024 * 1024),
        name="prepare",
    )(tokens, gain, info)


def branch_kernel(pieces, *refs):
    info_ref, mask_ref, normed_ref, strips_ref, late_ref = refs[:5]
    rims = refs[5 : 5 + ROUNDS]
    refs = refs[5 + ROUNDS :]
    mine, other = refs[:pieces], refs[pieces : 2 * pieces]
    refs = refs[2 * pieces :]
    far, far_other = refs[: pieces - 1], refs[pieces - 1 : 2 * pieces - 2]
    result_ref, rows_in, weights, keys, values, queries, mixed, out_ref, sems, row_sems, out_sems = refs[
        2 * pieces - 2 :
    ]
    core, group = info_ref[CORE], info_ref[GROUP]

    def weight_copies(half, near, beyond):
        for i in range(pieces):
            target = weights.at[half, pl.ds(pl.multiple_of(info_ref[PLACE + i], 16), near[i].shape[0])]
            if i == 0:
                yield pltpu.make_async_copy(near[0], target, sems.at[half, 0])
                continue
            start = pl.multiple_of(group * REST, LANES)
            part = target.at[:, pl.ds(start, PART)]
            yield pltpu.make_async_copy(near[i], part, sems.at[half, 2 * i])
            first = pl.multiple_of((1 - group) * (PART - REST), LANES)
            source = beyond[i - 1].at[:, pl.ds(first, REST)]
            rest = target.at[:, pl.ds(pl.multiple_of((1 - group) * PART, LANES), REST)]
            yield pltpu.make_async_copy(source, rest, sems.at[half, 2 * i - 1])

    def start_weights(half):
        @pl.when(core == half)
        def _():
            for copy in weight_copies(half, mine, far):
                copy.start()

        @pl.when(core != half)
        def _():
            for copy in weight_copies(half, other, far_other):
                copy.start()

    for slot in range(HOLD):

        @pl.when(info_ref[LIVE + slot] == 1)
        def _(slot=slot):
            target = rows_in.at[slot, pl.ds(0, ROWS), :]
            pltpu.make_async_copy(normed_ref.at[slot], target, row_sems.at[slot, 4]).start()

    busy = info_ref[LIVE] + info_ref[LIVE + 1] > 0

    @pl.when(busy)
    def _():
        start_weights(1)
        start_weights(0)

    for slot in range(HOLD):

        @pl.when(info_ref[LIVE + slot] == 1)
        def _(slot=slot):
            for side in range(4):
                source = info_ref[SOURCE + 4 * slot + side]
                span = pl.ds(ROWS + side * STRIP, STRIP)
                target = rows_in.at[slot, span, :]
                sem = row_sems.at[slot, side]
                for r in range(ROUNDS):

                    @pl.when(source == r)
                    def _(r=r, target=target, sem=sem):
                        pltpu.make_async_copy(rims[r], target, sem).start()

                @pl.when((source >= ROUNDS) & (source < MOST))
                def _(source=source, target=target, sem=sem):
                    pltpu.make_async_copy(late_ref.at[source - ROUNDS], target, sem).start()

                @pl.when((source >= LOCAL) & (source < NONE))
                def _(source=source, target=target, sem=sem):
                    pltpu.make_async_copy(strips_ref.at[source - LOCAL], target, sem).start()

                @pl.when(source == NONE)
                def _(slot=slot, span=span):
                    rows_in[slot, span, :] = jnp.zeros((STRIP, rows_in.shape[2]), BF)

    block = 512
    factor = math.log2(math.e) / math.sqrt(HS)
    dims = (((1,), (1,)), ((), ()))
    mixed[:, :LEAD] = jnp.zeros((ROWS, LEAD), BF)
    lane = lax.broadcasted_iota(jnp.int32, (KEYS, LANES), 1)
    one = jnp.where(lane == HS, 1.0, 0.0).astype(BF)
    for h in range(HEADS):
        queries[h] = one[:ROWS]
        values[h] = one

    def work(slot, _):
        live = info_ref[LIVE + slot] == 1

        @pl.when(live)
        def _():
            away = jnp.where(mask_ref[pl.ds(slot, 1), :] > 0.5, 0.0, -1e30)
            away = jnp.broadcast_to(away, (LANES, KEYS)).T
            away = jnp.where(lane == HS, away, 0.0).astype(BF)
            for h in range(HEADS):
                keys[h] = away
            initial = (slot == 0) | (info_ref[LIVE] == 0)

            def wait_weights(half):
                @pl.when(initial)
                def _():
                    for copy in weight_copies(half, mine, far):
                        copy.wait()

            target = rows_in.at[slot, pl.ds(0, ROWS), :]
            pltpu.make_async_copy(normed_ref.at[slot], target, row_sems.at[slot, 4]).wait()
            wait_weights(1)

            def make_queries(i, _):
                span = pl.ds(pl.multiple_of(i * block, block), block)
                total = jnp.dot(
                    rows_in[slot, span, :], weights[1, :, :HW], preferred_element_type=jnp.float32
                ).astype(BF)
                for h in range(HEADS):
                    queries[h, span, :HS] = total[:, h * HS : (h + 1) * HS]
                return 0

            lax.fori_loop(0, ROWS // block, make_queries, 0)
            for side in range(4):

                @pl.when(info_ref[SOURCE + 4 * slot + side] != NONE)
                def _(side=side):
                    target = rows_in.at[slot, pl.ds(ROWS + side * STRIP, STRIP), :]
                    pltpu.make_async_copy(rims[0], target, row_sems.at[slot, side]).wait()

            wait_weights(0)

            def make_keys(i, _):
                span = pl.ds(pl.multiple_of(i * block, block), block)
                total = jnp.dot(
                    rows_in[slot, span, :], weights[0], preferred_element_type=jnp.float32
                ).astype(BF)
                for h in range(HEADS):
                    keys[h, span, :HS] = total[:, h * HS : (h + 1) * HS]
                    values[h, span, :HS] = total[:, HW + h * HS : HW + (h + 1) * HS]
                return 0

            lax.fori_loop(0, KEYS // block, make_keys, 0)
            for h in range(HEADS):
                scores = lax.dot_general(
                    queries[h], keys[h], dims, preferred_element_type=jnp.float32
                )
                highest = jnp.max(scores, -1, keepdims=True)
                share = jnp.exp2((scores - highest) * factor).astype(BF)
                total = jnp.dot(share, values[h], preferred_element_type=jnp.float32)
                total = total[:, :HS] * (1.0 / total[:, HS : HS + 1])
                mixed[:, LEAD + h * HS : LEAD + (h + 1) * HS] = total.astype(BF)

            def project(i, _):
                span = pl.ds(pl.multiple_of(i * block, block), block)
                total = lax.dot_general(
                    mixed[span, :],
                    weights[1, :, HW - LEAD :],
                    dims,
                    preferred_element_type=jnp.float32,
                )
                out_ref[slot, span, :] = total.astype(BF)
                return 0

            lax.fori_loop(0, ROWS // block, project, 0)

        @pl.when(jnp.logical_not(live))
        def _():
            out_ref[slot] = jnp.zeros(out_ref.shape[1:], BF)

        leave(slot).start()
        return 0

    def leave(slot):
        return pltpu.make_async_copy(out_ref.at[slot], result_ref.at[slot], out_sems.at[slot])

    lax.fori_loop(0, HOLD, work, 0)
    for slot in range(HOLD):
        leave(slot).wait()


def branch(info, mask, normed, strips, late, rims, mine, other, far, far_other):
    width = normed.shape[2]
    pieces = len(mine)
    anywhere = pl.BlockSpec(memory_space=pl.ANY)
    vmem = pl.BlockSpec(memory_space=pltpu.VMEM)
    smem = pl.BlockSpec(memory_space=pltpu.SMEM)
    return pl.pallas_call(
        functools.partial(branch_kernel, pieces),
        out_shape=jax.ShapeDtypeStruct(normed.shape, BF),
        in_specs=[smem, vmem] + [anywhere] * (3 + ROUNDS + 4 * pieces - 2),
        out_specs=anywhere,
        scratch_shapes=[
            pltpu.VMEM((HOLD, KEYS, width), BF),
            pltpu.VMEM((2, width, 2 * HW), BF),
            pltpu.VMEM((HEADS, KEYS, LANES), BF),
            pltpu.VMEM((HEADS, KEYS, LANES), BF),
            pltpu.VMEM((HEADS, ROWS, LANES), BF),
            pltpu.VMEM((ROWS, LEAD + HW), BF),
            pltpu.VMEM(normed.shape, BF),
            pltpu.SemaphoreType.DMA((2, 2 * pieces)),
            pltpu.SemaphoreType.DMA((HOLD, 5)),
            pltpu.SemaphoreType.DMA((HOLD,)),
        ],
        compiler_params=pltpu.CompilerParams(vmem_limit_bytes=60 * 1024 * 1024),
        name="branch",
    )(info, mask, normed, strips, late, *rims, *mine, *other, *far, *far_other)


def unused(shape):
    def kernel(out_ref):
        pass

    return pl.pallas_call(
        kernel,
        out_shape=jax.ShapeDtypeStruct(shape, BF),
        out_specs=pl.BlockSpec(memory_space=pl.ANY),
        name="unused",
    )()


def meet(choice, block, count):
    def way(r):
        pairs = [(t, t ^ r) for t in range(count) if t ^ r < count]
        return lambda items: lax.ppermute(items[0], "tiles", pairs)

    ways = [lambda items: unused(items[0].shape)] + [way(r) for r in range(1, count)]
    return lax.switch(choice, ways, (block,))


def shards(tokens, padding, plan, neighbours, norm_gain, attention_weight, output_weight):
    count = lax.axis_size("tiles")
    chips = count // 2
    position = lax.axis_index("tiles")
    core = position % 2
    width = tokens.shape[2]
    rows = 2 * attention_weight.shape[0]
    info, mask = route(plan, neighbours, padding, rows)
    key_part = attention_weight[:, HW:]
    other_part = jnp.concatenate([attention_weight[:, :HW], output_weight.T], 1)

    def exchange(r, strips):
        block = lax.dynamic_index_in_dim(strips, info[SEND + r], 0, keepdims=False)
        return meet(info[MEET + r], block, count)

    def meet_round(r, sends):
        return meet(info[MEET + r], sends[r], count)

    if chips > 8:
        far, far_other = [], []
        normed, strips, *sends = prepare(tokens, norm_gain, info)
        rims = lax.map(lambda r: exchange(r, strips), jnp.arange(ROUNDS, dtype=jnp.int32))
        rims = [rims[r] for r in range(ROUNDS)]
        mine = [lax.all_gather(key_part, "tiles", axis=0, tiled=True)]
        other = [lax.all_gather(other_part, "tiles", axis=0, tiled=True)]
    else:
        order, forward = ring_pairs(count)
        backward = [(b, a) for a, b in forward]
        swap = [(t, t ^ 1) for t in range(count)]
        kept = jnp.where(core == 0, key_part, other_part)
        given = jnp.where(core == 0, other_part, key_part)
        peer = lax.ppermute(given, "tiles", swap)
        block = jnp.concatenate(
            [jnp.where(core == 0, kept, peer), jnp.where(core == 0, peer, kept)], 0
        )
        payload = jnp.where(lax.axis_index("groups") == 0, block[:, :PART], block[:, REST:])
        across = [(0, 1), (1, 0)]
        rims = []
        near, far, swapped = [block], [], {}
        ahead = behind = payload
        crossing, waiting = [], [("near", 0)]
        last = chips // 2
        step = 0
        while step < last or crossing or waiting:
            step += 1
            arrived, met = [], []
            if step <= last:
                ahead = lax.ppermute(ahead, "tiles", forward)
                arrived = [ahead]
                if 2 * step < chips:
                    behind = lax.ppermute(behind, "tiles", backward)
                    arrived += [behind]
            crossed = [lax.ppermute(near[i], "groups", across) for i in crossing]
            free = max(4 - len(arrived) - len(crossed), 0)
            turn, waiting = waiting[:free], waiting[free:]
            pool = {"near": near, "far": far}
            peers = [lax.ppermute(pool[kind][i], "tiles", swap) for kind, i in turn]
            if step == 1:
                normed, strips, *sends = prepare(tokens, norm_gain, info)
            elif step - 2 < ROUNDS:
                met = [meet_round(step - 2, sends)]
            arrived, sends, crossed, peers, met = lax.optimization_barrier(
                (arrived, sends, crossed, peers, met)
            )
            swapped.update(zip(turn, peers))
            waiting += [("far", len(far) + i) for i in range(len(crossed))]
            waiting += [("near", len(near) + i) for i in range(len(arrived))]
            crossing = range(len(near), len(near) + len(arrived))
            near += arrived
            far += crossed
            rims += met
            if step <= last:
                ahead, behind = arrived[0], arrived[-1]
        rims += [meet_round(r, sends) for r in range(len(rims), ROUNDS)]
        mine, other = near, [swapped["near", i] for i in range(len(near))]
        far_other = [swapped["far", i] for i in range(len(far))]

    late = lax.cond(
        info[LATE] == 1,
        lambda: lax.map(lambda r: exchange(r, strips), jnp.arange(ROUNDS, MOST, dtype=jnp.int32)),
        lambda: unused((MOST - ROUNDS, STRIP, width)),
    )
    return branch(info, mask, normed, strips, late, rims, mine, other, far, far_other)


def solution(mesh):
    return jax.shard_map(
        shards,
        mesh=mesh,
        in_specs=(
            P(("groups", "tiles"), None, None),
            P("groups", None),
            P("groups"),
            P("groups", None),
            P(),
            P("tiles", None),
            P(None, "tiles"),
        ),
        out_specs=P(("groups", "tiles"), None, None),
        check_vma=False,
    )
```

```python
import functools
import math

import jax
import jax.numpy as jnp
from jax import lax
from jax.experimental import pallas as pl
from jax.experimental.pallas import tpu as pltpu
from jax.sharding import PartitionSpec as P

HEADS = 8
HS = 104
HW = HEADS * HS
SIDE = 32
HALF = 16
RIM = 4
ROWS = 512
STRIP = 128
KEYS = ROWS + 4 * STRIP
HOLD = 2
LANES = 128
LEAD = 64
BF = jnp.bfloat16
PART = (2 * HW // LANES + 1) // 2 * LANES
REST = 2 * HW - PART

ROUNDS, MOST = 8, 15
MEET, SEND, SOURCE, LIVE, LATE, CORE, PLACE, GROUP, WHOLE = 0, 16, 32, 40, 42, 43, 44, 52, 53
LOCAL, NONE = 16, 32


def routing(count, rows, plan_ref, beside_ref, padding_ref, out_ref, mask_ref, live, used, color, tally, edges):
    me = lax.axis_index("tiles")
    slots = HOLD * count

    def clear(s, _):
        live[s] = 0
        return 0

    lax.fori_loop(0, slots, clear, 0, unroll=8)

    def mark(j, _):
        live[plan_ref[j]] = 1
        return 0

    lax.fori_loop(0, count, mark, 0, unroll=8)

    def empty(t, _):
        used[t] = 0
        return 0

    lax.fori_loop(0, count, empty, 0, unroll=8)

    for weight in range(3):
        tally[weight] = 0

    def collect(e, _):
        s = lax.shift_right_logical(e, 1)
        side = 1 + 2 * jnp.bitwise_and(e, 1)
        n = beside_ref[s, side]
        safe = jnp.maximum(n, 0)
        a, b = lax.shift_right_logical(s, 1), lax.shift_right_logical(safe, 1)

        @pl.when((n >= 0) & (a != b))
        def _():
            heavy = live[2 * a] * live[2 * a + 1] + live[2 * b] * live[2 * b + 1]
            place = tally[heavy]
            edges[2 * slots * heavy + place] = 4 * s + side
            tally[heavy] = place + 1

        return 0

    lax.fori_loop(0, 2 * slots, collect, 0, unroll=4)
    for weight in (2, 1, 0):

        def edge(e, _, weight=weight):
            key = edges[2 * slots * weight + e]
            s = lax.shift_right_logical(key, 2)
            side = jnp.bitwise_and(key, 3)
            n = beside_ref[s, side]
            a, b = lax.shift_right_logical(s, 1), lax.shift_right_logical(n, 1)
            taken = jnp.bitwise_or(used[a], used[b])
            first = lax.while_loop(
                lambda c: jnp.bitwise_and(lax.shift_right_logical(taken, c), 1) == 1,
                lambda c: c + 1,
                jnp.int32(0),
            )
            bit = lax.shift_left(jnp.int32(1), first)
            used[a] = jnp.bitwise_or(used[a], bit)
            used[b] = jnp.bitwise_or(used[b], bit)
            color[key] = first
            color[4 * n + jnp.bitwise_xor(side, 1)] = first
            return 0

        lax.fori_loop(0, tally[weight], edge, 0)

    for r in range(MOST + 1):
        out_ref[MEET + r] = 0
        out_ref[SEND + r] = 0
    out_ref[LATE] = 0
    out_ref[WHOLE] = 0
    for i in range(HOLD):
        slot = HOLD * me + i
        out_ref[LIVE + i] = live[slot]
        mask_ref[i : i + 1, :ROWS] = padding_ref[pl.ds(slot, 1), :].astype(jnp.float32)
        for side in range(4):
            n = beside_ref[slot, side]
            has = (n >= 0) & (live[slot] == 1)
            safe = jnp.maximum(n, 0)
            other = lax.shift_right_logical(safe, 1)
            away = has & (other != me)
            out_ref[SOURCE + 4 * i + side] = jnp.where(has, LOCAL + 4 * jnp.bitwise_and(safe, 1) + side, NONE)

            @pl.when(away)
            def _(i=i, side=side, slot=slot, other=other):
                c = color[4 * slot + side]
                out_ref[SOURCE + 4 * i + side] = c
                out_ref[MEET + c] = jnp.bitwise_xor(other, me)
                out_ref[SEND + c] = 4 * i + (side ^ 1)

                @pl.when(c >= ROUNDS)
                def _():
                    out_ref[LATE] = 1
                    out_ref[WHOLE] = 1

            @pl.when(has & (other == me))
            def _():
                out_ref[WHOLE] = 1

            row_live = padding_ref[pl.ds(safe, 1), :].astype(jnp.float32)
            if side < 2:
                token = lax.broadcasted_iota(jnp.int32, (ROWS, STRIP), 0)
                place = lax.broadcasted_iota(jnp.int32, (ROWS, STRIP), 1)
                band = 2 * RIM
                wanted = lax.shift_right_logical(place, 3) * SIDE + jnp.bitwise_and(place, band - 1)
                wanted = wanted + (SIDE - band if side == 0 else 0)
                chosen = jnp.where(token == wanted, 1.0, 0.0).astype(BF)
                strip = jnp.dot(row_live.astype(BF), chosen, preferred_element_type=jnp.float32)
            else:
                strip = row_live[:, ROWS - STRIP :] if side == 2 else row_live[:, :STRIP]
            begin = ROWS + side * STRIP
            mask_ref[i : i + 1, begin : begin + STRIP] = jnp.where(has, strip, 0.0)

    core = jnp.bitwise_and(me, 1)
    chip = lax.shift_right_logical(me, 1)
    chips = count // 2
    order, _ = ring_pairs(count)
    plan_of_ring = ring_steps(chips)
    out_ref[CORE] = core if len(plan_of_ring) > 1 else jnp.int32(0)
    out_ref[GROUP] = lax.axis_index("groups")
    for index, step in enumerate(plan_of_ring):
        start = jnp.int32(0)
        if len(plan_of_ring) > 1:
            for rank, c in enumerate(order):
                start = jnp.where(chip == c, order[(rank + step) % chips] * rows, start)
        out_ref[PLACE + index] = start


def ring_pairs(count):
    chips = count // 2
    order = list(range(0, chips, 2)) + list(range(chips - 1 - chips % 2, 0, -2))
    forward = []
    for index, chip in enumerate(order):
        after = order[(index + 1) % chips]
        forward += [(2 * chip + c, 2 * after + c) for c in range(2)]
    return order, forward


def ring_steps(chips):
    if chips > 8:
        return [0]
    pieces = [0]
    for step in range(1, chips // 2 + 1):
        pieces += [-step, step] if 2 * step < chips else [-step]
    return pieces


def route(plan, neighbours, padding, rows):
    count = plan.shape[0]
    smem = pl.BlockSpec(memory_space=pltpu.SMEM)
    vmem = pl.BlockSpec(memory_space=pltpu.VMEM)
    return pl.pallas_call(
        functools.partial(routing, count, rows),
        out_shape=(
            jax.ShapeDtypeStruct((64,), jnp.int32),
            jax.ShapeDtypeStruct((HOLD, KEYS), jnp.float32),
        ),
        in_specs=[smem] * 2 + [vmem],
        out_specs=(smem, vmem),
        scratch_shapes=[
            pltpu.SMEM((HOLD * count,), jnp.int32),
            pltpu.SMEM((count,), jnp.int32),
            pltpu.SMEM((4 * HOLD * count,), jnp.int32),
            pltpu.SMEM((3,), jnp.int32),
            pltpu.SMEM((6 * HOLD * count,), jnp.int32),
        ],
        name="routing",
    )(plan, neighbours, padding)


def prepare_kernel(tokens_ref, gain_ref, info_ref, normed_ref, strips_ref, *rest):
    sends, (work, normed, strips, in_sems, out_sems, send_sems) = rest[:ROUNDS], rest[ROUNDS:]
    gain = gain_ref[...][None, :]
    band = 2 * RIM
    lives = [info_ref[LIVE + slot] == 1 for slot in range(HOLD)]

    def fetch(slot):
        return pltpu.make_async_copy(tokens_ref.at[slot], work.at[slot], in_sems.at[slot])

    def keep(slot):
        return pltpu.make_async_copy(normed.at[slot], normed_ref.at[slot], out_sems.at[slot])

    def keep_strips():
        return pltpu.make_async_copy(strips, strips_ref, out_sems.at[HOLD])

    def send(r):
        return pltpu.make_async_copy(strips.at[info_ref[SEND + r]], sends[r], send_sems.at[r])

    def normal(values):
        offset = values - jnp.mean(values, -1, keepdims=True)
        spread = jnp.mean(offset * offset, -1, keepdims=True)
        return offset * lax.rsqrt(spread + 1e-06) * gain

    for slot in range(HOLD):

        @pl.when(lives[slot])
        def _(slot=slot):
            fetch(slot).start()

    for slot in range(HOLD):

        @pl.when(lives[slot])
        def _(slot=slot):
            fetch(slot).wait()

            def pair(i, _):
                lines = []
                for half in range(2):
                    span = pl.ds(pl.multiple_of((2 * i + half) * SIDE, SIDE), SIDE)
                    line = normal(work[slot, span, :].astype(jnp.float32))
                    normed[slot, span, :] = line.astype(BF)
                    lines.append(line)
                span = pl.ds(pl.multiple_of(i * 2 * band, 2 * band), 2 * band)
                last = jnp.concatenate([line[SIDE - band :] for line in lines], 0)
                first = jnp.concatenate([line[:band] for line in lines], 0)
                strips[4 * slot, span, :] = last.astype(BF)
                strips[4 * slot + 1, span, :] = first.astype(BF)
                return 0

            lax.fori_loop(0, HALF // 2, pair, 0, unroll=8)
            strips[4 * slot + 2] = normed[slot, ROWS - STRIP :, :]
            strips[4 * slot + 3] = normed[slot, :STRIP, :]
            keep(slot).start()

    whole = info_ref[WHOLE] == 1

    @pl.when(whole)
    def _():
        keep_strips().start()

    for r in range(ROUNDS):

        @pl.when(info_ref[MEET + r] != 0)
        def _(r=r):
            send(r).start()

    for r in range(ROUNDS):

        @pl.when(info_ref[MEET + r] != 0)
        def _(r=r):
            send(r).wait()

    @pl.when(whole)
    def _():
        keep_strips().wait()

    for slot in range(HOLD):

        @pl.when(lives[slot])
        def _(slot=slot):
            keep(slot).wait()


def prepare(tokens, gain, info):
    width = tokens.shape[-1]
    anywhere = pl.BlockSpec(memory_space=pl.ANY)
    vmem = pl.BlockSpec(memory_space=pltpu.VMEM)
    smem = pl.BlockSpec(memory_space=pltpu.SMEM)
    return pl.pallas_call(
        prepare_kernel,
        out_shape=(
            jax.ShapeDtypeStruct(tokens.shape, BF),
            jax.ShapeDtypeStruct((4 * HOLD, STRIP, width), BF),
        )
        + (jax.ShapeDtypeStruct((STRIP, width), BF),) * ROUNDS,
        in_specs=[anywhere, vmem, smem],
        out_specs=(anywhere,) * (2 + ROUNDS),
        scratch_shapes=[
            pltpu.VMEM(tokens.shape, BF),
            pltpu.VMEM(tokens.shape, BF),
            pltpu.VMEM((4 * HOLD, STRIP, width), BF),
            pltpu.SemaphoreType.DMA((HOLD,)),
            pltpu.SemaphoreType.DMA((HOLD + 1,)),
            pltpu.SemaphoreType.DMA((ROUNDS,)),
        ],
        compiler_params=pltpu.CompilerParams(vmem_limit_bytes=60 * 1024 * 1024),
        name="prepare",
    )(tokens, gain, info)


def branch_kernel(pieces, *refs):
    info_ref, mask_ref, normed_ref, strips_ref, late_ref = refs[:5]
    rims = refs[5 : 5 + ROUNDS]
    refs = refs[5 + ROUNDS :]
    mine, other = refs[:pieces], refs[pieces : 2 * pieces]
    refs = refs[2 * pieces :]
    far, far_other = refs[: pieces - 1], refs[pieces - 1 : 2 * pieces - 2]
    result_ref, rows_in, weights, keys, values, queries, mixed, out_ref, sems, row_sems, out_sems = refs[
        2 * pieces - 2 :
    ]
    core, group = info_ref[CORE], info_ref[GROUP]

    def weight_copies(half, near, beyond):
        for i in range(pieces):
            target = weights.at[half, pl.ds(pl.multiple_of(info_ref[PLACE + i], 16), near[i].shape[0])]
            if i == 0:
                yield pltpu.make_async_copy(near[0], target, sems.at[half, 0])
                continue
            start = pl.multiple_of(group * REST, LANES)
            part = target.at[:, pl.ds(start, PART)]
            yield pltpu.make_async_copy(near[i], part, sems.at[half, 2 * i])
            first = pl.multiple_of((1 - group) * (PART - REST), LANES)
            source = beyond[i - 1].at[:, pl.ds(first, REST)]
            rest = target.at[:, pl.ds(pl.multiple_of((1 - group) * PART, LANES), REST)]
            yield pltpu.make_async_copy(source, rest, sems.at[half, 2 * i - 1])

    def start_weights(half):
        @pl.when(core == half)
        def _():
            for copy in weight_copies(half, mine, far):
                copy.start()

        @pl.when(core != half)
        def _():
            for copy in weight_copies(half, other, far_other):
                copy.start()

    for slot in range(HOLD):

        @pl.when(info_ref[LIVE + slot] == 1)
        def _(slot=slot):
            target = rows_in.at[slot, pl.ds(0, ROWS), :]
            pltpu.make_async_copy(normed_ref.at[slot], target, row_sems.at[slot, 4]).start()

    busy = info_ref[LIVE] + info_ref[LIVE + 1] > 0

    @pl.when(busy)
    def _():
        start_weights(1)
        start_weights(0)

    for slot in range(HOLD):

        @pl.when(info_ref[LIVE + slot] == 1)
        def _(slot=slot):
            for side in range(4):
                source = info_ref[SOURCE + 4 * slot + side]
                span = pl.ds(ROWS + side * STRIP, STRIP)
                target = rows_in.at[slot, span, :]
                sem = row_sems.at[slot, side]
                for r in range(ROUNDS):

                    @pl.when(source == r)
                    def _(r=r, target=target, sem=sem):
                        pltpu.make_async_copy(rims[r], target, sem).start()

                @pl.when((source >= ROUNDS) & (source < MOST))
                def _(source=source, target=target, sem=sem):
                    pltpu.make_async_copy(late_ref.at[source - ROUNDS], target, sem).start()

                @pl.when((source >= LOCAL) & (source < NONE))
                def _(source=source, target=target, sem=sem):
                    pltpu.make_async_copy(strips_ref.at[source - LOCAL], target, sem).start()

                @pl.when(source == NONE)
                def _(slot=slot, span=span):
                    rows_in[slot, span, :] = jnp.zeros((STRIP, rows_in.shape[2]), BF)

    block = 512
    factor = math.log2(math.e) / math.sqrt(HS)
    dims = (((1,), (1,)), ((), ()))
    mixed[:, :LEAD] = jnp.zeros((ROWS, LEAD), BF)
    lane = lax.broadcasted_iota(jnp.int32, (KEYS, LANES), 1)
    one = jnp.where(lane == HS, 1.0, 0.0).astype(BF)
    for h in range(HEADS):
        queries[h] = one[:ROWS]
        values[h] = one

    def work(slot, _):
        live = info_ref[LIVE + slot] == 1

        @pl.when(live)
        def _():
            away = jnp.where(mask_ref[pl.ds(slot, 1), :] > 0.5, 0.0, -1e30)
            away = jnp.broadcast_to(away, (LANES, KEYS)).T
            away = jnp.where(lane == HS, away, 0.0).astype(BF)
            for h in range(HEADS):
                keys[h] = away
            initial = (slot == 0) | (info_ref[LIVE] == 0)

            def wait_weights(half):
                @pl.when(initial)
                def _():
                    for copy in weight_copies(half, mine, far):
                        copy.wait()

            target = rows_in.at[slot, pl.ds(0, ROWS), :]
            pltpu.make_async_copy(normed_ref.at[slot], target, row_sems.at[slot, 4]).wait()
            wait_weights(1)

            def make_queries(i, _):
                span = pl.ds(pl.multiple_of(i * block, block), block)
                total = jnp.dot(
                    rows_in[slot, span, :], weights[1, :, :HW], preferred_element_type=jnp.float32
                ).astype(BF)
                for h in range(HEADS):
                    queries[h, span, :HS] = total[:, h * HS : (h + 1) * HS]
                return 0

            lax.fori_loop(0, ROWS // block, make_queries, 0)
            for side in range(4):

                @pl.when(info_ref[SOURCE + 4 * slot + side] != NONE)
                def _(side=side):
                    target = rows_in.at[slot, pl.ds(ROWS + side * STRIP, STRIP), :]
                    pltpu.make_async_copy(rims[0], target, row_sems.at[slot, side]).wait()

            wait_weights(0)

            def make_keys(i, _):
                span = pl.ds(pl.multiple_of(i * block, block), block)
                total = jnp.dot(
                    rows_in[slot, span, :], weights[0], preferred_element_type=jnp.float32
                ).astype(BF)
                for h in range(HEADS):
                    keys[h, span, :HS] = total[:, h * HS : (h + 1) * HS]
                    values[h, span, :HS] = total[:, HW + h * HS : HW + (h + 1) * HS]
                return 0

            lax.fori_loop(0, KEYS // block, make_keys, 0)
            for h in range(HEADS):
                scores = lax.dot_general(
                    queries[h], keys[h], dims, preferred_element_type=jnp.float32
                )
                highest = jnp.max(scores, -1, keepdims=True)
                share = jnp.exp2((scores - highest) * factor).astype(BF)
                total = jnp.dot(share, values[h], preferred_element_type=jnp.float32)
                total = total[:, :HS] * (1.0 / total[:, HS : HS + 1])
                mixed[:, LEAD + h * HS : LEAD + (h + 1) * HS] = total.astype(BF)

            def project(i, _):
                span = pl.ds(pl.multiple_of(i * block, block), block)
                total = lax.dot_general(
                    mixed[span, :],
                    weights[1, :, HW - LEAD :],
                    dims,
                    preferred_element_type=jnp.float32,
                )
                out_ref[slot, span, :] = total.astype(BF)
                return 0

            lax.fori_loop(0, ROWS // block, project, 0)

        @pl.when(jnp.logical_not(live))
        def _():
            out_ref[slot] = jnp.zeros(out_ref.shape[1:], BF)

        leave(slot).start()
        return 0

    def leave(slot):
        return pltpu.make_async_copy(out_ref.at[slot], result_ref.at[slot], out_sems.at[slot])

    lax.fori_loop(0, HOLD, work, 0)
    for slot in range(HOLD):
        leave(slot).wait()


def branch(info, mask, normed, strips, late, rims, mine, other, far, far_other):
    width = normed.shape[2]
    pieces = len(mine)
    anywhere = pl.BlockSpec(memory_space=pl.ANY)
    vmem = pl.BlockSpec(memory_space=pltpu.VMEM)
    smem = pl.BlockSpec(memory_space=pltpu.SMEM)
    return pl.pallas_call(
        functools.partial(branch_kernel, pieces),
        out_shape=jax.ShapeDtypeStruct(normed.shape, BF),
        in_specs=[smem, vmem] + [anywhere] * (3 + ROUNDS + 4 * pieces - 2),
        out_specs=anywhere,
        scratch_shapes=[
            pltpu.VMEM((HOLD, KEYS, width), BF),
            pltpu.VMEM((2, width, 2 * HW), BF),
            pltpu.VMEM((HEADS, KEYS, LANES), BF),
            pltpu.VMEM((HEADS, KEYS, LANES), BF),
            pltpu.VMEM((HEADS, ROWS, LANES), BF),
            pltpu.VMEM((ROWS, LEAD + HW), BF),
            pltpu.VMEM(normed.shape, BF),
            pltpu.SemaphoreType.DMA((2, 2 * pieces)),
            pltpu.SemaphoreType.DMA((HOLD, 5)),
            pltpu.SemaphoreType.DMA((HOLD,)),
        ],
        compiler_params=pltpu.CompilerParams(vmem_limit_bytes=60 * 1024 * 1024),
        name="branch",
    )(info, mask, normed, strips, late, *rims, *mine, *other, *far, *far_other)


def unused(shape):
    def kernel(out_ref):
        pass

    return pl.pallas_call(
        kernel,
        out_shape=jax.ShapeDtypeStruct(shape, BF),
        out_specs=pl.BlockSpec(memory_space=pl.ANY),
        name="unused",
    )()


def meet(choice, block, count):
    def way(r):
        pairs = [(t, t ^ r) for t in range(count) if t ^ r < count]
        return lambda items: lax.ppermute(items[0], "tiles", pairs)

    ways = [lambda items: unused(items[0].shape)] + [way(r) for r in range(1, count)]
    return lax.switch(choice, ways, (block,))


def shards(tokens, padding, plan, neighbours, norm_gain, attention_weight, output_weight):
    count = lax.axis_size("tiles")
    chips = count // 2
    position = lax.axis_index("tiles")
    core = position % 2
    width = tokens.shape[2]
    rows = 2 * attention_weight.shape[0]
    info, mask = route(plan, neighbours, padding, rows)
    key_part = attention_weight[:, HW:]
    other_part = jnp.concatenate([attention_weight[:, :HW], output_weight.T], 1)

    def exchange(r, strips):
        block = lax.dynamic_index_in_dim(strips, info[SEND + r], 0, keepdims=False)
        return meet(info[MEET + r], block, count)

    def meet_round(r, sends):
        return meet(info[MEET + r], sends[r], count)

    if chips > 8:
        far, far_other = [], []
        normed, strips, *sends = prepare(tokens, norm_gain, info)
        rims = lax.map(lambda r: exchange(r, strips), jnp.arange(ROUNDS, dtype=jnp.int32))
        rims = [rims[r] for r in range(ROUNDS)]
        mine = [lax.all_gather(key_part, "tiles", axis=0, tiled=True)]
        other = [lax.all_gather(other_part, "tiles", axis=0, tiled=True)]
    else:
        order, forward = ring_pairs(count)
        backward = [(b, a) for a, b in forward]
        swap = [(t, t ^ 1) for t in range(count)]
        kept = jnp.where(core == 0, key_part, other_part)
        given = jnp.where(core == 0, other_part, key_part)
        peer = lax.ppermute(given, "tiles", swap)
        block = jnp.concatenate(
            [jnp.where(core == 0, kept, peer), jnp.where(core == 0, peer, kept)], 0
        )
        payload = jnp.where(lax.axis_index("groups") == 0, block[:, :PART], block[:, REST:])
        across = [(0, 1), (1, 0)]
        rims = []
        near, far, swapped = [block], [], {}
        ahead = behind = payload
        crossing, waiting = [], [("near", 0)]
        last = chips // 2
        step = 0
        while step < last or crossing or waiting:
            step += 1
            arrived, met = [], []
            if step <= last:
                ahead = lax.ppermute(ahead, "tiles", forward)
                arrived = [ahead]
                if 2 * step < chips:
                    behind = lax.ppermute(behind, "tiles", backward)
                    arrived += [behind]
            crossed = [lax.ppermute(near[i], "groups", across) for i in crossing]
            free = max(4 - len(arrived) - len(crossed), 0)
            turn, waiting = waiting[:free], waiting[free:]
            pool = {"near": near, "far": far}
            peers = [lax.ppermute(pool[kind][i], "tiles", swap) for kind, i in turn]
            if step == 1:
                normed, strips, *sends = prepare(tokens, norm_gain, info)
            elif step - 2 < ROUNDS:
                met = [meet_round(step - 2, sends)]
            arrived, sends, crossed, peers, met = lax.optimization_barrier(
                (arrived, sends, crossed, peers, met)
            )
            swapped.update(zip(turn, peers))
            waiting += [("far", len(far) + i) for i in range(len(crossed))]
            waiting += [("near", len(near) + i) for i in range(len(arrived))]
            crossing = range(len(near), len(near) + len(arrived))
            near += arrived
            far += crossed
            rims += met
            if step <= last:
                ahead, behind = arrived[0], arrived[-1]
        rims += [meet_round(r, sends) for r in range(len(rims), ROUNDS)]
        mine, other = near, [swapped["near", i] for i in range(len(near))]
        far_other = [swapped["far", i] for i in range(len(far))]

    late = lax.cond(
        info[LATE] == 1,
        lambda: lax.map(lambda r: exchange(r, strips), jnp.arange(ROUNDS, MOST, dtype=jnp.int32)),
        lambda: unused((MOST - ROUNDS, STRIP, width)),
    )
    return branch(info, mask, normed, strips, late, rims, mine, other, far, far_other)


def solution(mesh):
    return jax.shard_map(
        shards,
        mesh=mesh,
        in_specs=(
            P(("groups", "tiles"), None, None),
            P("groups", None),
            P("groups"),
            P("groups", None),
            P(),
            P("tiles", None),
            P(None, "tiles"),
        ),
        out_specs=P(("groups", "tiles"), None, None),
        check_vma=False,
    )
```
